256 devices in a mesh: gx: 16 (over x, y), gy: 8 (over z_hi, core), gz: 2 (over z_lo).
Axes of the slice: x: 4, y: 4, z: 8 (z_hi: 4, z_lo: 2; z = z_hi * 2 + z_lo), core: 2. Of those that a mesh axis runs over, the one named last changes fastest.
Arguments:
- density: float32 [8, 1024, 2048], P('gz', 'gx', 'gy'), may hold values from 0.01 to 0.05
- tap_index: int32 [8, 16, 16, 128], P('gz', 'gx', 'gy'), may hold values from 0 to 8191
- tap_current: float32 [8, 16, 16, 128], P('gz', 'gx', 'gy'), may hold values from 0.5 to 4
- pad_cond: float32 [8, 1024, 2048], P('gz', 'gx', 'gy'), may hold values from 0.05 to 0.5
- row_cond: float32 [8, 1024, 2048], P('gz', 'gx', 'gy'), may hold values from 0.5 to 1.2
- col_cond: float32 [8, 1024, 2048], P('gz', 'gx', 'gy'), may hold values from 1 to 2
- material: int32 [8, 1024, 2048], P('gz', 'gx', 'gy'), may hold values from 0 to 3
- leak_rates: float32 [4], replicated, may hold values from 0.5 to 4
- theta_start: float32 [32, 1024, 2048], P(None, 'gx', ('gy', 'gz')), may hold values from -6 to 6
- kappa: float32 [32, 1024, 2048], P(None, 'gx', ('gy', 'gz')), may hold values from 1 to 2
- inv_capacity: float32 [32, 1024, 2048], P(None, 'gx', ('gy', 'gz')), may hold values from 0.04 to 0.08
Outputs:
- ir_drop: float32 [8, 1024, 2048], P('gz', 'gx', 'gy')
- temperature: float32 [32, 1024, 2048], P(None, 'gx', ('gy', 'gz'))
The draws below stay inside these ranges and needn't reach their ends.
All inputs are finite; a program needn't handle non-finite values.
Results may differ from the reference program's by a relative error of at most 0.00002.
Values sent between devices are 32-bit elements; how exact they have to be, the bound alone decides.
A program may use at most 128 MiB of HBM per device.

```python
import math
import jax
import jax.numpy as jnp

TIERS = 8
LAYERS_TIER = 4
MATERIALS = 4
SWEEPS = 16
STEPS = 4
TX = 64
TY = 128
TAPS = 128
NX = 1024
NY = 2048
NZ = 32


def log_between(key, shape, low, high):
    return jnp.exp(jax.random.uniform(key, shape, jnp.float32, math.log(low), math.log(high)))


def draw_pad_cond(key, part):
    key = jax.random.fold_in(key, 21)
    shape = (TIERS, NX, NY)
    return log_between(key, shape, 0.05, 0.5)


def draw_row_cond(key, part):
    key = jax.random.fold_in(key, 22)
    shape = (TIERS, NX, NY)
    return log_between(key, shape, 0.5, 1.2)


def draw_col_cond(key, part):
    key = jax.random.fold_in(key, 23)
    shape = (TIERS, NX, NY)
    return log_between(key, shape, 1.0, 2.0)


def draw_theta_start(key, part):
    key = jax.random.fold_in(key, 24)
    shape = (NZ, NX, NY)
    return jnp.clip(1.5 * jax.random.normal(key, shape, jnp.float32), -6.0, 6.0)


def draw_kappa(key, part):
    key = jax.random.fold_in(key, 25)
    shape = (NZ, NX, NY)
    return log_between(key, shape, 1.0, 2.0)


def draw_inv_capacity(key, part):
    key = jax.random.fold_in(key, 26)
    shape = (NZ, NX, NY)
    return log_between(key, shape, 0.04, 0.08)


def place_ends(values, own_key, smallest, largest):
    longest = values.shape.index(max(values.shape))
    spots = []
    for shift in (0, 1):
        where = [jax.random.randint(jax.random.fold_in(own_key, axis), (), 0, length) for axis, length in enumerate(values.shape)]
        where[longest] = (where[longest] + shift) % values.shape[longest]
        spots.append(tuple(where))
    return values.at[spots[0]].set(smallest).at[spots[1]].set(largest)


def levels(key, extent, cuts, smallest, top_value):
    gain, own = 1.0, jax.random.fold_in(key, 6)
    for dim, shards_of in cuts:
        heights = jnp.exp(jax.random.uniform(jax.random.fold_in(own, dim), (shards_of,), jnp.float32, smallest / len(cuts), top_value / len(cuts)))
        gain = gain * jnp.repeat(heights, extent[dim] // shards_of).reshape([-1 if axis == dim else 1 for axis in range(len(extent))])
    return gain


def setup_inputs(seed: int = 0) -> dict:
    splits = jax.random.split(jax.random.key(seed), 12)
    return {
        "density": jnp.clip(jnp.exp(math.log(0.05) - 1.609438 * jax.random.uniform(splits[0], (TIERS, NX, NY), jnp.float32) ** levels(splits[0], (TIERS, NX, NY), ((0, 2), (1, 16), (2, 8)), -0.2, 0.2)), 0.01, 0.05),
        "tap_index": place_ends(jax.random.randint(splits[1], (TIERS, NX // TX, NY // TY, TAPS), 0, TX * TY), jax.random.fold_in(splits[1], 1), 0, (TX * TY) - 1).astype(jnp.int32),
        "tap_current": jnp.clip(jnp.exp(math.log(4.0) - 2.0794415 * jax.random.uniform(splits[2], (TIERS, NX // TX, NY // TY, TAPS), jnp.float32) ** levels(splits[2], (TIERS, NX // TX, NY // TY, TAPS), ((0, 2), (1, 16), (2, 8)), -0.2, 0.2)), 0.5, 4.0),
        "pad_cond": draw_pad_cond(jax.random.fold_in(splits[11], 71), 0),
        "row_cond": draw_row_cond(jax.random.fold_in(splits[11], 71), 0),
        "col_cond": draw_col_cond(jax.random.fold_in(splits[11], 71), 0),
        "material": place_ends(jax.random.randint(splits[6], (TIERS, NX, NY), 0, MATERIALS), jax.random.fold_in(splits[6], 1), 0, MATERIALS - 1).astype(jnp.int32),
        "leak_rates": jnp.clip(jnp.exp(jax.random.uniform(splits[7], (MATERIALS,), jnp.float32, math.log(0.5), math.log(4.0))), 0.5, 4.0),
        "theta_start": draw_theta_start(jax.random.fold_in(splits[11], 71), 0),
        "kappa": draw_kappa(jax.random.fold_in(splits[11], 71), 0),
        "inv_capacity": draw_inv_capacity(jax.random.fold_in(splits[11], 71), 0),
    }


def place_taps(tap_current, tap_index, tiers, rows, cols):
    blocks_x = rows // TX
    blocks_y = cols // TY
    base = (jnp.arange(tiers * blocks_x * blocks_y, dtype=jnp.int32) * (TX * TY)).reshape(tiers, blocks_x, blocks_y, 1)
    flat_index = (base + tap_index.astype(jnp.int32)).reshape(-1)
    summed = jnp.zeros((tiers * blocks_x * blocks_y * TX * TY,), jnp.float32).at[flat_index].add(tap_current.reshape(-1))
    summed = summed.reshape(tiers, blocks_x, blocks_y, TX, TY).transpose(0, 1, 3, 2, 4)
    return summed.reshape(tiers, rows, cols)


def relax(source, gxp, gxm, gyp, gym, denom, padded):
    beside_all = gxp * padded[:, 2:, 1:-1] + gxm * padded[:, :-2, 1:-1]
    beside_all = beside_all + gyp * padded[:, 1:-1, 2:] + gym * padded[:, 1:-1, :-2]
    return (source + beside_all) / denom


def harmonic(first, second):
    return 2.0 * first * second / (first + second)


def heat_step(theta, padded, links, inv_capacity, heat):
    kxn, kxp, kyn, kyp, kzu, kzd = links
    zero_layer = jnp.zeros_like(theta[:1])
    upper = jnp.concatenate([theta[1:], zero_layer], 0)
    lower = jnp.concatenate([zero_layer, theta[:-1]], 0)
    flow = kxn * (padded[:, 2:, 1:-1] - theta) + kxp * (padded[:, :-2, 1:-1] - theta)
    flow = flow + kyn * (padded[:, 1:-1, 2:] - theta) + kyp * (padded[:, 1:-1, :-2] - theta)
    flow = flow + kzu * (upper - theta) + kzd * (lower - theta)
    return theta + inv_capacity * (flow + heat)


def vertical_links(kappa):
    inner = harmonic(kappa[:-1], kappa[1:])
    kzu = jnp.concatenate([inner, jnp.zeros_like(kappa[:1])], 0)
    kzd = jnp.concatenate([kappa[:1], inner], 0)
    return kzu, kzd


def leakage(material, leak_rates, drop):
    leak = jnp.zeros(drop.shape, jnp.float32)
    for kind in range(MATERIALS):
        leak = leak + jnp.where(material == kind, leak_rates[kind], 0.0)
    return leak * jnp.exp(-drop)


def reference(density, tap_index, tap_current, pad_cond, row_cond, col_cond, material, leak_rates, theta_start, kappa, inv_capacity):
    source = density + place_taps(tap_current, tap_index, TIERS, NX, NY)
    gxp = row_cond.at[:, -1, :].set(0.0)
    gyp = col_cond.at[:, :, -1].set(0.0)
    gxm = jnp.concatenate([jnp.zeros_like(gxp[:, :1]), gxp[:, :-1]], 1)
    gym = jnp.concatenate([jnp.zeros_like(gyp[:, :, :1]), gyp[:, :, :-1]], 2)
    denom = pad_cond + gxp + gxm + gyp + gym
    drop = jnp.zeros_like(source)
    for sweep in range(SWEEPS):
        padded = jnp.pad(drop, ((0, 0), (1, 1), (1, 1)))
        drop = relax(source, gxp, gxm, gyp, gym, denom, padded)
    next_row = jnp.concatenate([drop[:, 1:], jnp.zeros_like(drop[:, :1])], 1)
    next_col = jnp.concatenate([drop[:, :, 1:], jnp.zeros_like(drop[:, :, :1])], 2)
    row_diff = next_row - drop
    col_diff = next_col - drop
    power = pad_cond * drop * drop + gxp * row_diff * row_diff + gyp * col_diff * col_diff
    power = power + leakage(material, leak_rates, drop)
    heat = jnp.concatenate([power[:, None], jnp.zeros((TIERS, LAYERS_TIER - 1, NX, NY), jnp.float32)], 1).reshape(NZ, NX, NY)
    kpad = jnp.pad(kappa, ((0, 0), (1, 1), (1, 1)))
    kzu, kzd = vertical_links(kappa)
    links = (harmonic(kappa, kpad[:, 2:, 1:-1]), harmonic(kappa, kpad[:, :-2, 1:-1]), harmonic(kappa, kpad[:, 1:-1, 2:]), harmonic(kappa, kpad[:, 1:-1, :-2]), kzu, kzd)
    theta = theta_start
    for step in range(STEPS):
        padded = jnp.pad(theta, ((0, 0), (1, 1), (1, 1)))
        theta = heat_step(theta, padded, links, inv_capacity, heat)
    return drop, theta
```

```python
import functools

import jax
import jax.numpy as jnp
from jax import lax
from jax.experimental import pallas as pl
from jax.experimental.pallas import tpu as pltpu
from jax.sharding import PartitionSpec as P

MESH = pl.DeviceIdType.MESH
F32 = jnp.float32
SWEEPS = 16
STEPS = 4
MATERIALS = 4
HALO = 20
PITCH = 24
TOP = 24
V = 13
W = 9
SRC, PAD, GXP, GYP, LEAK = range(5)
DIRS = ((-1, 0), (1, 0), (0, -1), (0, 1), (-1, -1), (-1, 1), (1, -1), (1, 1))


def iota(shape, dim):
    return lax.broadcasted_iota(jnp.int32, shape, dim)


def roll(x, shift, axis):
    return pltpu.roll(x, shift % x.shape[axis], axis)


def inverse(x):
    r = pl.reciprocal(x, approx=True)
    r = r * (2.0 - x * r)
    return r * (2.0 - x * r)


def harmonic(a, b):
    return 2.0 * a * b * inverse(a + b)


def mesh_kernel(
    sizes,
    tidx, tcur, dens, pad, row, col, mat, rates, theta, kappa, invc,
    drop_out, heat_out, trow, tx, ty,
    ext, row_send, row_recv, col_send, xr, yr, coef, raw, usave, nat, unat, trow_send, tcol_send, heat_send,
    ssem, rsem, tssem, trsem, pssem, prsem,
):
    nx, ny, nz = sizes
    gx, gy, gz = lax.axis_index("gx"), lax.axis_index("gy"), lax.axis_index("gz")
    tiers, rows, cols = dens.shape
    nc = ny * nz
    c = gy * nz + gz

    def mesh_to(d):
        dx, dy = DIRS[d]
        return (lax.rem(gx + dx + nx, nx), lax.rem(gy + dy + ny, ny), gz)

    def heat_to(d):
        dx, dy = DIRS[d]
        there = lax.rem(c + dy + nc, nc)
        return (lax.rem(gx + dx + nx, nx), there // nz, lax.rem(there, nz))

    partner = (gx, gy, 1 - gz)

    barrier = pltpu.get_barrier_semaphore()
    for d in range(8):
        pl.semaphore_signal(barrier, inc=1, device_id=mesh_to(d), device_id_type=MESH)
    for d in range(2, 8):
        pl.semaphore_signal(barrier, inc=1, device_id=heat_to(d), device_id_type=MESH)

    def mesh_copy(d, t):
        top, bottom = pl.ds(0, TOP), pl.ds(rows - TOP, TOP)
        if d < 2:
            src, dst = row_send.at[d, t], row_recv.at[d, t]
        elif d == 2:
            src, dst = col_send.at[0, t], xr.at[t, pl.ds(TOP, rows)]
        elif d == 3:
            src, dst = col_send.at[1, t], yr.at[t, pl.ds(TOP, rows)]
        elif d == 4:
            src, dst = col_send.at[0, t, top], xr.at[t, pl.ds(TOP + rows, TOP)]
        elif d == 5:
            src, dst = col_send.at[1, t, top], yr.at[t, pl.ds(TOP + rows, TOP)]
        elif d == 6:
            src, dst = col_send.at[0, t, bottom], xr.at[t, pl.ds(0, TOP)]
        else:
            src, dst = col_send.at[1, t, bottom], yr.at[t, pl.ds(0, TOP)]
        return pltpu.make_async_remote_copy(
            src_ref=src, dst_ref=dst, send_sem=ssem.at[d, t], recv_sem=rsem.at[d, t],
            device_id=mesh_to(d), device_id_type=MESH,
        )

    def heat_copy(d):
        top, bottom = pl.ds(0, 8), pl.ds(rows - 8, 8)
        if d < 2:
            src, dst = trow_send.at[d], trow.at[d]
        elif d == 2:
            src, dst = tcol_send.at[0], tx.at[:, pl.ds(8, rows)]
        elif d == 3:
            src, dst = tcol_send.at[1], ty.at[:, pl.ds(8, rows)]
        elif d == 4:
            src, dst = tcol_send.at[0, :, top], tx.at[:, pl.ds(8 + rows, 8)]
        elif d == 5:
            src, dst = tcol_send.at[1, :, top], ty.at[:, pl.ds(8 + rows, 8)]
        elif d == 6:
            src, dst = tcol_send.at[0, :, bottom], tx.at[:, pl.ds(0, 8)]
        else:
            src, dst = tcol_send.at[1, :, bottom], ty.at[:, pl.ds(0, 8)]
        return pltpu.make_async_remote_copy(
            src_ref=src, dst_ref=dst, send_sem=tssem.at[d], recv_sem=trsem.at[d],
            device_id=heat_to(d), device_id_type=MESH,
        )

    def power_copy(t):
        return pltpu.make_async_remote_copy(
            src_ref=heat_send.at[t], dst_ref=heat_out.at[gz * tiers + t], send_sem=pssem.at[t], recv_sem=prsem.at[t],
            device_id=partner, device_id_type=MESH,
        )

    def prepare(t):
        idx, cur = tidx[t], tcur[t]
        tiles = []
        for b in range(2):
            spot = idx[b : b + 1]
            at_row = jnp.where(iota((rows, 128), 0) == (spot >> 7), cur[b : b + 1], 0.0)
            at_col = jnp.where(iota((128, 128), 0) == (spot & 127), 1.0, 0.0)
            tiles.append(lax.dot_general(
                at_row, at_col, (((1,), (1,)), ((), ())),
                precision=lax.Precision.HIGHEST, preferred_element_type=F32,
            ))
        source = dens[t] + jnp.concatenate(tiles, 1)
        last_row = (iota((rows, cols), 0) == rows - 1) & (gx == nx - 1)
        last_col = (iota((rows, cols), 1) == cols - 1) & (gy == ny - 1)
        gxp = jnp.where(last_row, 0.0, row[t])
        gyp = jnp.where(last_col, 0.0, col[t])
        kinds = mat[t]
        leak = jnp.zeros((rows, cols), F32)
        for kind in range(MATERIALS):
            leak = jnp.where(kinds == kind, rates[kind], leak)
        fields = (source, pad[t], gxp, gyp, leak)
        lane = iota((rows, 128), 1)
        left = right = jnp.zeros((rows, 128), F32)
        for a, field in enumerate(fields):
            for tile in range(2):
                ext[a, t, tile, pl.ds(TOP, rows), :] = field[:, tile * 128 : tile * 128 + 128]
            size = HALO if a < LEAK else 4
            at = a * HALO if a < LEAK else LEAK * HALO
            row_send[0, t, at : at + size, :] = field[:size]
            row_send[1, t, at : at + size, :] = field[rows - size :]
            mine = (lane >= a * PITCH) & (lane < a * PITCH + size)
            left = jnp.where(mine, roll(field[:, :128], a * PITCH, 1), left)
            right = jnp.where(mine, roll(field[:, cols - 128 :], a * PITCH + size, 1), right)
        row_send[0, t, 84:88, :] = jnp.zeros((4, cols), F32)
        row_send[1, t, 84:88, :] = jnp.zeros((4, cols), F32)
        col_send[0, t] = left
        col_send[1, t] = right

    def pack_heat():
        sub = iota((16, 8, 128), 1)
        lane = iota((rows, 128), 1)
        for a, field in enumerate((theta, kappa, invc)):
            one, two = field[0:16, 0:8, :], field[16:32, 0:8, :]
            trow_send[0, a] = jnp.where(sub < 4, one, roll(two, 4, 1))
            one, two = field[0:16, rows - 8 : rows, :], field[16:32, rows - 8 : rows, :]
            trow_send[1, a] = jnp.where(sub < 4, roll(one, 4, 1), two)

            def gather(l, held):
                low, high = held
                mine = (lane >> 3) == l
                shift = lax.rem(8 * l + 4, 128)
                low = jnp.where(mine, pltpu.roll(field[l], shift, 1), low)
                high = jnp.where(mine, pltpu.roll(field[l + 16], shift, 1), high)
                return low, high

            zero = jnp.zeros((rows, 128), F32)
            low, high = lax.fori_loop(0, 16, gather, (zero, zero))
            first = (lane & 7) < 4
            tcol_send[0, a] = jnp.where(first, roll(high, -4, 1), low)
            tcol_send[1, a] = jnp.where(first, low, roll(high, 4, 1))

    def first_tiers(t, carry):
        prepare(t)

        @pl.when(t == 0)
        def _():
            pl.semaphore_wait(barrier, 14)

        for d in range(8):
            mesh_copy(d, t).start()
        return carry

    lax.fori_loop(0, tiers, first_tiers, 0)
    pack_heat()
    for d in range(8):
        heat_copy(d).start()

    lane_ext = iota((8, 384), 1)
    inside = (lane_ext < cols + HALO) | (lane_ext >= 384 - HALO)
    lane = iota((rows + 2 * TOP, 128), 1)
    half = iota((8, 128), 1) < 64

    def tier(t, carry):
        for d in range(8):
            mesh_copy(d, t).wait_recv()
        for a in range(5):
            size = HALO if a < LEAK else 4
            at = a * HALO if a < LEAK else LEAK * HALO
            for tile in range(2):
                part = pl.ds(tile * 128, 128)
                ext[a, t, tile, 0:TOP, :] = jnp.zeros((TOP, 128), F32)
                ext[a, t, tile, TOP - size : TOP, :] = row_recv[1, t, at : at + size, part]
                ext[a, t, tile, TOP + rows :, :] = jnp.zeros((TOP, 128), F32)
                ext[a, t, tile, TOP + rows : TOP + rows + size, :] = row_recv[0, t, at : at + size, part]
            ext[a, t, 2] = jnp.where(
                lane < 64, roll(xr[t], -a * PITCH, 1), roll(yr[t], 128 - size - a * PITCH, 1)
            )

        def load(a, start):
            return jnp.concatenate([ext[a, t, tile, pl.ds(start, 8, stride=V), :] for tile in range(3)], 1)

        def coefficients(v, held):
            start = TOP - HALO + v
            fields = [load(a, start) for a in range(5)]
            src, pd, gxp, gyp, leak = fields
            gxm = load(GXP, start - 1)
            gym = roll(gyp, 1, 1)
            r = jnp.where(inside, inverse(pd + gxp + gxm + gyp + gym), 0.0)
            for i, x in enumerate((src, gxp, gxm, gyp, gym)):
                coef[i, v] = x * r
            for i, x in enumerate((pd, gxp, gyp, leak)):
                raw[i, v] = x
            return held

        lax.fori_loop(0, V, coefficients, 0)

        def next_row(u):
            return jnp.concatenate([u[1:], roll(u[:1], -1, 1)], 0)

        def sweep(count, u):
            below = next_row(u)
            above = jnp.concatenate([roll(u[-1:], 1, 1), u[:-1]], 0)
            flow = coef[1] * below + coef[2] * above
            flow = flow + coef[3] * roll(u, -1, 2) + coef[4] * roll(u, 1, 2)
            return coef[0] + flow

        u = lax.fori_loop(0, SWEEPS - 1, sweep, coef[0])
        across, along = next_row(u) - u, roll(u, -1, 2) - u
        power = raw[0] * u * u + raw[1] * across * across + raw[2] * along * along + raw[3] * jnp.exp(-u)
        usave[0] = u
        usave[1] = power

        def spread(v, held):
            at = pl.ds(TOP - HALO + v, 8, stride=V)
            for tile in range(3):
                if tile < 2:
                    unat[tile, at, :] = usave[0, v, :, tile * 128 : tile * 128 + 128]
                nat[tile, at, :] = usave[1, v, :, tile * 128 : tile * 128 + 128]
            return held

        lax.fori_loop(0, V, spread, 0)
        for tile in range(2):
            drop_out[t, :, tile * 128 : tile * 128 + 128] = unat[tile, TOP : TOP + rows, :]

        def hand(v, held):
            at = pl.ds(TOP - 4 + v, 8, stride=W)

            def pair(z):
                return nat[z, at, :], jnp.where(half, nat[1 + z, at, :], nat[2 - 2 * z, at, :])

            heat_send[t, 0, v], heat_send[t, 1, v] = pair(1 - gz)
            heat_out[gz * tiers + t, 0, v], heat_out[gz * tiers + t, 1, v] = pair(gz)
            return held

        lax.fori_loop(0, W, hand, 0)
        power_copy(t).start()
        return carry

    lax.fori_loop(0, tiers, tier, 0)

    def finish(t, carry):
        for d in range(8):
            mesh_copy(d, t).wait_send()
        pltpu.make_async_remote_copy(
            src_ref=heat_send.at[t], dst_ref=heat_out.at[(1 - gz) * tiers + t], send_sem=pssem.at[t],
            recv_sem=prsem.at[t], device_id=partner, device_id_type=MESH,
        ).wait()
        return carry

    lax.fori_loop(0, tiers, finish, 0)
    for d in range(8):
        heat_copy(d).wait()


def heat_kernel(sizes, theta, kappa, invc, heat, trow, tx, ty, out, nat, temp, cap, lx, ly, lz, onat):
    nx, ny, nz = sizes
    layers, rows, lanes = theta.shape
    gx = lax.axis_index("gx")
    c = lax.axis_index("gy") * nz + lax.axis_index("gz")
    lane = iota((rows + 16, 128), 1)
    first = (lane & 7) < 4

    for a, field in enumerate((theta, kappa, invc)):
        x, y = tx[a], ty[a]
        packs = (jnp.where(first, y, x), jnp.where(first, roll(y, -4, 1), roll(x, 4, 1)))
        for part, pack in enumerate(packs):

            def unpack(l, held, a=a, field=field, part=part, pack=pack):
                layer = part * 16 + l
                above, below = trow[1, a, l], trow[0, a, l]
                nat[a, layer, 0, 0:8, :] = above if part else roll(above, 4, 0)
                nat[a, layer, 0, pl.ds(8, rows), :] = field[layer]
                nat[a, layer, 0, pl.ds(8 + rows, 8), :] = roll(below, 4, 0) if part else below
                nat[a, layer, 1] = pltpu.roll(pack, lax.rem(252 - 8 * l, 128), 1)
                return held

            lax.fori_loop(0, 16, unpack, 0)

    shape = (W, 8, 2 * lanes)
    row_of = iota(shape, 1) * W + iota(shape, 0) - 4
    col_of = iota(shape, 2)
    no_row = ((row_of == rows - 1) & (gx == nx - 1)) | ((row_of == -1) & (gx == 0))
    no_col = ((col_of == lanes - 1) & (c == ny * nz - 1)) | ((col_of == 2 * lanes - 1) & (c == 0))

    def strided(a, layer):
        return jnp.stack([
            jnp.concatenate([nat[a, layer, tile, pl.ds(4 + v, 8, stride=W), :] for tile in range(2)], 1)
            for v in range(W)
        ])

    def next_row(x):
        return jnp.concatenate([x[1:], roll(x[:1], -1, 1)], 0)

    def last_row(x):
        return jnp.concatenate([roll(x[-1:], 1, 1), x[:-1]], 0)

    def links(layer, k):
        temp[layer] = strided(0, layer)
        cap[layer] = strided(2, layer)
        lx[layer] = jnp.where(no_row, 0.0, harmonic(k, next_row(k)))
        ly[layer] = jnp.where(no_col, 0.0, harmonic(k, roll(k, -1, 2)))
        over = strided(1, jnp.minimum(layer + 1, layers - 1))
        lz[layer + 1] = jnp.where(layer == layers - 1, 0.0, harmonic(k, over))
        return over

    ground = strided(1, 0)
    lz[0] = ground
    lax.fori_loop(0, layers, links, ground)

    def step(count, carry):
        def per_tier(tier, below):
            for part in range(4):
                layer = tier * 4 + part
                here = temp[layer]
                fx = lx[layer] * (next_row(here) - here)
                fy = ly[layer] * (roll(here, -1, 2) - here)
                fz = lz[layer + 1] * (temp[jnp.minimum(layer + 1, layers - 1)] - here)
                flow = (fx - last_row(fx)) + (fy - roll(fy, 1, 2)) + (fz - below)
                if part == 0:
                    flow = flow + jnp.concatenate([heat[tier, 0], heat[tier, 1]], 2)
                temp[layer] = here + cap[layer] * flow
                below = fz
            return below

        lax.fori_loop(0, layers // 4, per_tier, lz[0] * temp[0])
        return carry

    lax.fori_loop(0, STEPS, step, 0)

    def result(layer, carry):
        for v in range(W):
            onat[pl.ds(4 + v, 8, stride=W), :] = temp[layer, v, :, 0:lanes]
        out[layer] = onat[pl.ds(8, rows), :]
        return carry

    lax.fori_loop(0, layers, result, 0)


def shards(sizes, density, tap_index, tap_current, pad_cond, row_cond, col_cond, material, leak_rates, theta, kappa, invc):
    tiers, rows, cols = density.shape
    layers, _, lanes = theta.shape
    vmem = pl.BlockSpec(memory_space=pltpu.VMEM)
    tall = rows + 2 * TOP
    dma = pltpu.SemaphoreType.DMA
    taps = tap_index.shape[-1]
    drop, heat, trow, tx, ty = pl.pallas_call(
        functools.partial(mesh_kernel, sizes),
        out_shape=(
            jax.ShapeDtypeStruct((tiers, rows, cols), F32),
            jax.ShapeDtypeStruct((2 * tiers, 2, W, 8, 128), F32),
            jax.ShapeDtypeStruct((2, 3, 16, 8, 128), F32),
            jax.ShapeDtypeStruct((3, rows + 16, 128), F32),
            jax.ShapeDtypeStruct((3, rows + 16, 128), F32),
        ),
        in_specs=[vmem] * 7 + [pl.BlockSpec(memory_space=pltpu.SMEM)] + [vmem] * 3,
        out_specs=(vmem,) * 5,
        scratch_shapes=[
            pltpu.VMEM((5, tiers, 3, tall, 128), F32),
            pltpu.VMEM((2, tiers, 88, cols), F32),
            pltpu.VMEM((2, tiers, 88, cols), F32),
            pltpu.VMEM((2, tiers, rows, 128), F32),
            pltpu.VMEM((tiers, tall, 128), F32),
            pltpu.VMEM((tiers, tall, 128), F32),
            pltpu.VMEM((5, V, 8, 384), F32),
            pltpu.VMEM((4, V, 8, 384), F32),
            pltpu.VMEM((2, V, 8, 384), F32),
            pltpu.VMEM((3, tall, 128), F32),
            pltpu.VMEM((2, tall, 128), F32),
            pltpu.VMEM((2, 3, 16, 8, 128), F32),
            pltpu.VMEM((2, 3, rows, 128), F32),
            pltpu.VMEM((tiers, 2, W, 8, 128), F32),
            dma((8, tiers)), dma((8, tiers)), dma((8,)), dma((8,)), dma((tiers,)), dma((tiers,)),
        ],
        compiler_params=pltpu.CompilerParams(
            collective_id=0, has_side_effects=True, vmem_limit_bytes=48 * 2**20
        ),
        name="mesh_sweeps",
    )(
        tap_index.reshape(tiers, 2, taps), tap_current.reshape(tiers, 2, taps), density, pad_cond, row_cond, col_cond,
        material, leak_rates, theta, kappa, invc,
    )
    block = (W, 8, 2 * lanes)
    temperature = pl.pallas_call(
        functools.partial(heat_kernel, sizes),
        out_shape=jax.ShapeDtypeStruct(theta.shape, F32),
        in_specs=[vmem] * 7,
        out_specs=vmem,
        scratch_shapes=[
            pltpu.VMEM((3, layers, 2, rows + 16, 128), F32),
            pltpu.VMEM((layers, *block), F32),
            pltpu.VMEM((layers, *block), F32),
            pltpu.VMEM((layers, *block), F32),
            pltpu.VMEM((layers, *block), F32),
            pltpu.VMEM((layers + 1, *block), F32),
            pltpu.VMEM((rows + 16, 128), F32),
        ],
        compiler_params=pltpu.CompilerParams(vmem_limit_bytes=48 * 2**20),
        name="heat_steps",
    )(theta, kappa, invc, heat, trow, tx, ty)
    return drop, temperature


def solution(mesh):
    sizes = tuple(mesh.shape[name] for name in ("gx", "gy", "gz"))
    field = P("gz", "gx", "gy")
    tap = P("gz", "gx", "gy", None)
    block = P(None, "gx", ("gy", "gz"))
    return jax.shard_map(
        functools.partial(shards, sizes),
        mesh=mesh,
        in_specs=(field, tap, tap, field, field, field, field, P(), block, block, block),
        out_specs=(field, block),
        check_vma=False,
    )
```

```python
import functools

import jax
import jax.numpy as jnp
from jax import lax
from jax.experimental import pallas as pl
from jax.experimental.pallas import tpu as pltpu
from jax.sharding import PartitionSpec as P

MESH = pl.DeviceIdType.MESH
F32 = jnp.float32
SWEEPS = 16
STEPS = 4
MATERIALS = 4
HALO = 20
PITCH = 24
TOP = 24
V = 13
W = 9
SRC, PAD, GXP, GYP, LEAK = range(5)
DIRS = ((-1, 0), (1, 0), (0, -1), (0, 1), (-1, -1), (-1, 1), (1, -1), (1, 1))


def iota(shape, dim):
    return lax.broadcasted_iota(jnp.int32, shape, dim)


def roll(x, shift, axis):
    return pltpu.roll(x, shift % x.shape[axis], axis)


def harmonic(a, b):
    total = a + b
    r = pl.reciprocal(total, approx=True)
    r = r * (2.0 - total * r)
    r = r * (2.0 - total * r)
    return 2.0 * a * b * r


def inverse_root(x):
    r = lax.rsqrt(x)
    return r * (1.5 - 0.5 * x * r * r)


def next_row(x):
    return jnp.concatenate([x[1:], roll(x[:1], -1, 1)], 0)


def last_row(x):
    return jnp.concatenate([roll(x[-1:], 1, 1), x[:-1]], 0)


def kernel(
    sizes,
    tidx_hbm, tcur_hbm, dens_hbm, pad_hbm, row_hbm, col_hbm, mat_hbm, rates, theta_hbm, kappa_hbm, invc_hbm,
    drop_out, temp_out,
    tidx, tcur, mat, ext, row_send, row_recv, col_send, xr, yr, coef, raw, ub, nat, unat,
    field, trow_send, trow, tcol_send, tx, ty, edge, heat_send, heat,
    temp, cap, lx, ly, lz, snat, stemp, scap, slx, sly, slz, sground, sheat, mix, onat,
    isem, ssem, rsem, tssem, trsem, pssem, prsem,
):
    nx, ny, nz = sizes
    gx, gy, gz = lax.axis_index("gx"), lax.axis_index("gy"), lax.axis_index("gz")
    tiers, rows, cols = drop_out.shape
    layers = temp_out.shape[0]
    nc = ny * nz
    c = gy * nz + gz

    loads = [pltpu.make_async_copy(tidx_hbm, tidx, isem.at[0]), pltpu.make_async_copy(tcur_hbm, tcur, isem.at[1])]
    for a, ref in enumerate((dens_hbm, pad_hbm, row_hbm, col_hbm)):
        for tile in range(2):
            loads.append(pltpu.make_async_copy(
                ref.at[:, :, pl.ds(tile * 128, 128)], ext.at[a, :, tile, pl.ds(TOP, rows)], isem.at[len(loads)]
            ))
    loads.append(pltpu.make_async_copy(mat_hbm, mat, isem.at[len(loads)]))
    heat_loads = [
        pltpu.make_async_copy(ref, field.at[a, :, pl.ds(8, rows)], isem.at[len(loads) + a])
        for a, ref in enumerate((theta_hbm, kappa_hbm, invc_hbm))
    ]
    for load in loads + heat_loads:
        load.start()

    def mesh_to(d):
        dx, dy = DIRS[d]
        return (lax.rem(gx + dx + nx, nx), lax.rem(gy + dy + ny, ny), gz)

    def heat_to(d):
        dx, dy = DIRS[d]
        there = lax.rem(c + dy + nc, nc)
        return (lax.rem(gx + dx + nx, nx), there // nz, lax.rem(there, nz))

    partner = (gx, gy, 1 - gz)

    barrier = pltpu.get_barrier_semaphore()
    for d in range(8):
        pl.semaphore_signal(barrier, inc=1, device_id=mesh_to(d), device_id_type=MESH)
    for d in range(2, 8):
        pl.semaphore_signal(barrier, inc=1, device_id=heat_to(d), device_id_type=MESH)

    def mesh_copy(d, t):
        top, bottom = pl.ds(0, TOP), pl.ds(rows - TOP, TOP)
        if d < 2:
            src, dst = row_send.at[d, t], row_recv.at[d, t]
        elif d == 2:
            src, dst = col_send.at[0, t], xr.at[t, pl.ds(TOP, rows)]
        elif d == 3:
            src, dst = col_send.at[1, t], yr.at[t, pl.ds(TOP, rows)]
        elif d == 4:
            src, dst = col_send.at[0, t, top], xr.at[t, pl.ds(TOP + rows, TOP)]
        elif d == 5:
            src, dst = col_send.at[1, t, top], yr.at[t, pl.ds(TOP + rows, TOP)]
        elif d == 6:
            src, dst = col_send.at[0, t, bottom], xr.at[t, pl.ds(0, TOP)]
        else:
            src, dst = col_send.at[1, t, bottom], yr.at[t, pl.ds(0, TOP)]
        return pltpu.make_async_remote_copy(
            src_ref=src, dst_ref=dst, send_sem=ssem.at[d, t], recv_sem=rsem.at[d, t],
            device_id=mesh_to(d), device_id_type=MESH,
        )

    def heat_copy(d):
        top, bottom = pl.ds(0, 8), pl.ds(rows - 8, 8)
        if d < 2:
            src, dst = trow_send.at[d], trow.at[d]
        elif d == 2:
            src, dst = tcol_send.at[0], tx.at[:, pl.ds(8, rows)]
        elif d == 3:
            src, dst = tcol_send.at[1], ty.at[:, pl.ds(8, rows)]
        elif d == 4:
            src, dst = tcol_send.at[0, :, top], tx.at[:, pl.ds(8 + rows, 8)]
        elif d == 5:
            src, dst = tcol_send.at[1, :, top], ty.at[:, pl.ds(8 + rows, 8)]
        elif d == 6:
            src, dst = tcol_send.at[0, :, bottom], tx.at[:, pl.ds(0, 8)]
        else:
            src, dst = tcol_send.at[1, :, bottom], ty.at[:, pl.ds(0, 8)]
        return pltpu.make_async_remote_copy(
            src_ref=src, dst_ref=dst, send_sem=tssem.at[d], recv_sem=trsem.at[d],
            device_id=heat_to(d), device_id_type=MESH,
        )

    def power_copy(t, z):
        return pltpu.make_async_remote_copy(
            src_ref=heat_send.at[t], dst_ref=heat.at[z * tiers + t], send_sem=pssem.at[t], recv_sem=prsem.at[t],
            device_id=partner, device_id_type=MESH,
        )

    def prepare(t):
        idx, cur = tidx[t], tcur[t]
        main = pl.ds(TOP, rows)
        lane = iota((rows, 128), 1)
        end_row = (iota((rows, 128), 0) == rows - 1) & (gx == nx - 1)
        end_col = (lane == 127) & (gy == ny - 1)
        edges = []
        for tile in range(2):
            spot = idx[tile : tile + 1]
            at_row = jnp.where(iota((rows, 128), 0) == (spot >> 7), cur[tile : tile + 1], 0.0)
            at_col = jnp.where(iota((128, 128), 0) == (spot & 127), 1.0, 0.0)
            taps = lax.dot_general(
                at_row, at_col, (((1,), (1,)), ((), ())),
                precision=lax.Precision.HIGHEST, preferred_element_type=F32,
            )
            source = ext[SRC, t, tile, main, :] + taps
            pad = ext[PAD, t, tile, main, :]
            gxp = jnp.where(end_row, 0.0, ext[GXP, t, tile, main, :])
            gyp = ext[GYP, t, tile, main, :]
            if tile == 1:
                gyp = jnp.where(end_col, 0.0, gyp)
            kinds = mat[t, :, tile * 128 : tile * 128 + 128]
            leak = jnp.zeros((rows, 128), F32)
            for kind in range(MATERIALS):
                leak = jnp.where(kinds == kind, rates[kind], leak)
            ext[SRC, t, tile, main, :] = source
            ext[GXP, t, tile, main, :] = gxp
            ext[GYP, t, tile, main, :] = gyp
            ext[LEAK, t, tile, main, :] = leak
            packed = jnp.zeros((rows, 128), F32)
            part = pl.ds(tile * 128, 128)
            for a, values in enumerate((source, pad, gxp, gyp, leak)):
                size = HALO if a < LEAK else 4
                at = a * HALO if a < LEAK else LEAK * HALO
                row_send[0, t, at : at + size, part] = values[:size]
                row_send[1, t, at : at + size, part] = values[rows - size :]
                mine = (lane >= a * PITCH) & (lane < a * PITCH + size)
                packed = jnp.where(mine, roll(values, a * PITCH + (size if tile else 0), 1), packed)
            row_send[0, t, 84:88, part] = jnp.zeros((4, 128), F32)
            row_send[1, t, 84:88, part] = jnp.zeros((4, 128), F32)
            col_send[tile, t] = packed

    def first_tiers(t, carry):
        prepare(t)

        @pl.when(t == 0)
        def _():
            pl.semaphore_wait(barrier, 14)

        for d in range(8):
            mesh_copy(d, t).start()
        return carry

    for load in loads:
        load.wait()
    lax.fori_loop(0, tiers, first_tiers, 0)

    lane_tall = iota((rows, 128), 1)
    sub = iota((16, 8, 128), 1)
    main = pl.ds(8, rows)
    for load in heat_loads:
        load.wait()
    for a in range(3):
        one, two = field[a, 0:16, 8:16, :], field[a, 16:32, 8:16, :]
        trow_send[0, a] = jnp.where(sub < 4, one, roll(two, 4, 1))
        one, two = field[a, 0:16, rows : rows + 8, :], field[a, 16:32, rows : rows + 8, :]
        trow_send[1, a] = jnp.where(sub < 4, roll(one, 4, 1), two)

    def gather(a, carry):
        low = high = jnp.zeros((rows, 128), F32)
        for l in range(16):
            mine = (lane_tall >> 3) == l
            low = jnp.where(mine, roll(field[a, l, main, :], 8 * l + 4, 1), low)
            high = jnp.where(mine, roll(field[a, l + 16, main, :], 8 * l + 4, 1), high)
        first = (lane_tall & 4) == 0
        tcol_send[0, a] = jnp.where(first, roll(high, -4, 1), low)
        tcol_send[1, a] = jnp.where(first, low, roll(high, 4, 1))
        edge[a, 0, main, :] = low
        edge[a, 1, main, :] = high
        return carry

    lax.fori_loop(0, 3, gather, 0)
    for d in range(8):
        heat_copy(d).start()

    lane_ext = iota((8, 384), 1)
    inside = (lane_ext < cols + HALO) | (lane_ext >= 384 - HALO)
    lane_rows = iota((rows + 2 * TOP, 128), 1)
    half = iota((8, 128), 1) < 64

    def tier(t, carry):
        for d in range(8):
            mesh_copy(d, t).wait_recv()
        for a in range(5):
            size = HALO if a < LEAK else 4
            at = a * HALO if a < LEAK else LEAK * HALO
            for tile in range(2):
                part = pl.ds(tile * 128, 128)
                ext[a, t, tile, 0:8, :] = jnp.zeros((8, 128), F32)
                ext[a, t, tile, TOP - size : TOP, :] = row_recv[1, t, at : at + size, part]
                ext[a, t, tile, TOP + rows : TOP + rows + size, :] = row_recv[0, t, at : at + size, part]
                if a == LEAK:
                    ext[a, t, tile, 8 : TOP - size, :] = jnp.zeros((TOP - size - 8, 128), F32)
                    ext[a, t, tile, TOP + rows + size :, :] = jnp.zeros((TOP - size, 128), F32)
            ext[a, t, 2] = jnp.where(
                lane_rows < 64, roll(xr[t], -a * PITCH, 1), roll(yr[t], 128 - size - a * PITCH, 1)
            )

        def fetch(a, start):
            return jnp.concatenate([ext[a, t, tile, pl.ds(start, 8, stride=V), :] for tile in range(3)], 1)

        roots, gxm = [], fetch(GXP, TOP - HALO - 1)
        for v in range(V):
            src, pd, gxp, gyp, leak = [fetch(a, TOP - HALO + v) for a in range(5)]
            r = jnp.where(inside, inverse_root(pd + gxp + gxm + gyp + roll(gyp, 1, 1)), 0.0)
            gxm = gxp
            for i, x in enumerate((pd, gxp, gyp, leak, r)):
                raw[i, v] = x
            coef[0, v] = src * r
            coef[2, v] = gyp * r * roll(r, -1, 1)
        for v in range(V):
            after = raw[4, v + 1] if v < V - 1 else roll(raw[4, 0], -1, 0)
            coef[1, v] = raw[1, v] * raw[4, v] * after
        coef[1, V] = roll(coef[1, V - 1], 1, 0)

        def sweep(source_of, out):
            here = source_of(0)
            before, link_before = roll(source_of(V - 1), 1, 0), coef[1, V]
            for v in range(V):
                after = source_of(v + 1) if v < V - 1 else roll(source_of(0), -1, 0)
                link, side = coef[1, v], coef[2, v]
                flow = link * after + link_before * before
                flow = flow + (side * roll(here, -1, 1) + roll(side * here, 1, 1))
                ub[out, v] = coef[0, v] + flow
                before, here, link_before = here, after, link

        sweep(lambda v: coef[0, v], 0)

        def two_sweeps(count, held):
            sweep(lambda v: ub[0, v], 1)
            sweep(lambda v: ub[1, v], 0)
            return held

        lax.fori_loop(0, (SWEEPS - 2) // 2, two_sweeps, 0)
        here = first = ub[0, 0] * raw[4, 0]
        for v in range(V):
            after = ub[0, v + 1] * raw[4, v + 1] if v < V - 1 else roll(first, -1, 0)
            across, along = after - here, roll(here, -1, 1) - here
            power = raw[0, v] * here * here + raw[1, v] * across * across + raw[2, v] * along * along
            power = power + raw[3, v] * jnp.exp(-here)
            at = pl.ds(TOP - HALO + v, 8, stride=V)
            for tile in range(3):
                nat[tile, at, :] = power[:, tile * 128 : tile * 128 + 128]
                if tile < 2:
                    unat[tile, at, :] = here[:, tile * 128 : tile * 128 + 128]
            here = after

        for v in range(W):
            at = pl.ds(TOP - 4 + v, 8, stride=W)
            for z, into in ((1 - gz, heat_send.at[t]), (gz, heat.at[gz * tiers + t])):
                into[0, v] = nat[z, at, :]
                into[1, v] = jnp.where(half, nat[1 + z, at, :], nat[2 - 2 * z, at, :])
        power_copy(t, gz).start()
        for tile in range(2):
            drop_out[t, :, tile * 128 : tile * 128 + 128] = unat[tile, TOP : TOP + rows, :]
        return carry

    lax.fori_loop(0, tiers, tier, 0)

    for d in range(8):
        heat_copy(d).wait_recv()
    lane8 = iota((8, 128), 1)
    lane_tall = iota((rows + 16, 128), 1)
    first = (lane_tall & 4) == 0

    def assemble(a, carry):
        above, below = trow[1, a], trow[0, a]
        field[a, 0:16, 0:8, :] = roll(above, 4, 1)
        field[a, 16:32, 0:8, :] = above
        field[a, 0:16, 8 + rows : 16 + rows, :] = below
        field[a, 16:32, 8 + rows : 16 + rows, :] = roll(below, 4, 1)
        up = down = jnp.zeros((8, 128), F32)
        for l in range(16):
            mine = (lane8 >> 3) == l
            up = jnp.where(mine, roll(above[l], 8 * l + 4, 1), up)
            down = jnp.where(mine, roll(below[l], 8 * l + 4, 1), down)
        edge[a, 0, 0:8, :] = roll(up, 4, 0)
        edge[a, 1, 0:8, :] = up
        edge[a, 0, 8 + rows : 16 + rows, :] = down
        edge[a, 1, 8 + rows : 16 + rows, :] = roll(down, 4, 0)
        x, y, low, high = tx[a], ty[a], edge[a, 0], edge[a, 1]
        snat[a, 0] = jnp.where(first, y, low)
        snat[a, 1] = jnp.where(first, low, x)
        snat[a, 2] = jnp.where(first, roll(y, -4, 1), high)
        snat[a, 3] = jnp.where(first, high, roll(x, 4, 1))
        return carry

    lax.fori_loop(0, 3, assemble, 0)

    shape = (W, 8, 128)
    row_of = iota(shape, 1) * W + iota(shape, 0) - 4
    lane = iota(shape, 2)
    no_row = ((row_of == rows - 1) & (gx == nx - 1)) | ((row_of == -1) & (gx == 0))
    no_col = (lane == 127) & (c == nc - 1)

    def strided(ref):
        return jnp.stack([ref[pl.ds(4 + v, 8, stride=W), :] for v in range(W)])

    def upper(low, high):
        return jnp.where(lane < 120, roll(low, -8, 2), roll(high, -8, 2)), roll(high, -8, 2)

    def align(x, layer):
        return pltpu.roll(x, lax.rem(252 - 8 * lax.rem(layer, 16), 128), 2)

    for side in range(2):
        k = [strided(snat.at[1, 2 * h + side]) for h in range(2)]
        over = upper(*k)
        no_edge = ((lane & 7) == 3) & (c == (nc - 1 if side else 0))
        sground[side] = k[0]
        for h in range(2):
            s = 2 * h + side
            stemp[s] = strided(snat.at[0, s])
            scap[s] = strided(snat.at[2, s])
            slx[s] = jnp.where(no_row, 0.0, harmonic(k[h], next_row(k[h])))
            sly[s] = jnp.where(no_edge, 0.0, harmonic(k[h], roll(k[h], -1, 2)))
            link = harmonic(k[h], over[h])
            slz[s] = jnp.where(lane < 120, link, 0.0) if h else link
            if side:
                mix[h] = k[h]

    def links(layer, k):
        temp[layer] = strided(field.at[0, layer])
        cap[layer] = strided(field.at[2, layer])
        over = strided(field.at[1, jnp.minimum(layer + 1, layers - 1)])
        beside = roll(jnp.where(lane == 0, align(mix[layer // 16], layer), k), -1, 2)
        lx[layer] = jnp.where(no_row, 0.0, harmonic(k, next_row(k)))
        ly[layer] = jnp.where(no_col, 0.0, harmonic(k, beside))
        lz[layer + 1] = jnp.where(layer == layers - 1, 0.0, harmonic(k, over))
        return over

    ground = strided(field.at[1, 0])
    lz[0] = ground
    lax.fori_loop(0, layers, links, ground)

    for t in range(tiers):
        power_copy(t, 1 - gz).wait()

    for h in range(2):
        left = right = jnp.zeros(shape, F32)
        for t in range(4):
            inner, outer = heat[h * 4 + t, 0], heat[h * 4 + t, 1]
            mine = (lane >> 3) == 4 * t
            left = jnp.where(mine, roll(jnp.where(lane < 64, inner, outer), 32 * t + 4, 2), left)
            right = jnp.where(mine, roll(jnp.where(lane < 64, outer, inner), 32 * t + 4, 2), right)
        sheat[2 * h] = left
        sheat[2 * h + 1] = right

    def step(count, carry):
        for side in range(2):
            old = [stemp[side], stemp[2 + side]]
            over = upper(*old)
            rise = [slz[2 * h + side] * (over[h] - old[h]) for h in range(2)]
            under = (
                jnp.where(lane < 8, sground[side] * old[0], roll(rise[0], 8, 2)),
                jnp.where(lane < 8, roll(rise[0], 8, 2), roll(rise[1], 8, 2)),
            )
            for h in range(2):
                s = 2 * h + side
                here = old[h]
                fx = slx[s] * (next_row(here) - here)
                fy = sly[s] * (roll(here, -1, 2) - here)
                flow = (fx - last_row(fx)) + (fy - roll(fy, 1, 2)) + (rise[h] - under[h]) + sheat[s]
                stemp[s] = here + scap[s] * flow
                mix[h] = jnp.where((lane & 7) == 3, mix[h], here) if side else fy

        def per_tier(tier, below):
            for part in range(4):
                layer = tier * 4 + part
                here = temp[layer]
                beyond = align(mix[tier // 4], layer)
                fx = lx[layer] * (next_row(here) - here)
                fy = ly[layer] * (roll(jnp.where(lane == 0, beyond, here), -1, 2) - here)
                fz = lz[layer + 1] * (temp[jnp.minimum(layer + 1, layers - 1)] - here)
                before = roll(jnp.where(lane == 127, beyond, fy), 1, 2)
                flow = (fx - last_row(fx)) + (fy - before) + (fz - below)
                if part == 0:
                    flow = flow + heat[tier, 0]
                temp[layer] = here + cap[layer] * flow
                below = fz
            return below

        lax.fori_loop(0, layers // 4, per_tier, lz[0] * temp[0])
        return carry

    lax.fori_loop(0, STEPS, step, 0)

    def result(layer, carry):
        for v in range(W):
            onat[layer, pl.ds(4 + v, 8, stride=W), :] = temp[layer, v]
        temp_out[layer] = onat[layer, pl.ds(8, rows), :]
        return carry

    lax.fori_loop(0, layers, result, 0, unroll=4)

    def finish(t, carry):
        for d in range(8):
            mesh_copy(d, t).wait_send()
        return carry

    lax.fori_loop(0, tiers, finish, 0)
    for d in range(8):
        heat_copy(d).wait_send()


def shards(sizes, density, tap_index, tap_current, pad_cond, row_cond, col_cond, material, leak_rates, theta, kappa, invc):
    tiers, rows, cols = density.shape
    layers = theta.shape[0]
    vmem, hbm = pl.BlockSpec(memory_space=pltpu.VMEM), pl.BlockSpec(memory_space=pl.ANY)
    tall, high = rows + 2 * TOP, rows + 16
    dma = pltpu.SemaphoreType.DMA
    taps = tap_index.shape[-1]
    scratch = [
        (5, tiers, 3, tall, 128),
        (2, tiers, 88, cols), (2, tiers, 88, cols), (2, tiers, rows, 128),
        (tiers, tall, 128), (tiers, tall, 128),
        (3, V + 1, 8, 384), (5, V, 8, 384), (2, V, 8, 384),
        (3, tall, 128), (2, tall, 128),
        (3, layers, high, 128),
        (2, 3, 16, 8, 128), (2, 3, 16, 8, 128),
        (2, 3, rows, 128), (3, high, 128), (3, high, 128), (3, 2, high, 128),
        (tiers, 2, W, 8, 128), (2 * tiers, 2, W, 8, 128),
        (layers, W, 8, 128), (layers, W, 8, 128),
        (layers, W, 8, 128), (layers, W, 8, 128), (layers + 1, W, 8, 128),
        (3, 4, high, 128),
        (4, W, 8, 128), (4, W, 8, 128), (4, W, 8, 128), (4, W, 8, 128), (4, W, 8, 128),
        (2, W, 8, 128), (4, W, 8, 128), (2, W, 8, 128),
        (layers, high, 128),
    ]
    return pl.pallas_call(
        functools.partial(kernel, sizes),
        out_shape=(jax.ShapeDtypeStruct((tiers, rows, cols), F32), jax.ShapeDtypeStruct(theta.shape, F32)),
        in_specs=[hbm] * 7 + [pl.BlockSpec(memory_space=pltpu.SMEM)] + [hbm] * 3,
        out_specs=(vmem, vmem),
        scratch_shapes=[
            pltpu.VMEM((tiers, 2, taps), jnp.int32),
            pltpu.VMEM((tiers, 2, taps), F32),
            pltpu.VMEM((tiers, rows, cols), jnp.int32),
            *[pltpu.VMEM(size, F32) for size in scratch],
            dma((14,)), dma((8, tiers)), dma((8, tiers)), dma((8,)), dma((8,)), dma((tiers,)), dma((tiers,)),
        ],
        compiler_params=pltpu.CompilerParams(
            collective_id=0, has_side_effects=True, vmem_limit_bytes=56 * 2**20
        ),
        name="electrothermal",
    )(
        tap_index.reshape(tiers, 2, taps), tap_current.reshape(tiers, 2, taps), density, pad_cond, row_cond, col_cond,
        material, leak_rates, theta, kappa, invc,
    )


def solution(mesh):
    sizes = tuple(mesh.shape[name] for name in ("gx", "gy", "gz"))
    mesh_field = P("gz", "gx", "gy")
    tap = P("gz", "gx", "gy", None)
    block = P(None, "gx", ("gy", "gz"))
    return jax.shard_map(
        functools.partial(shards, sizes),
        mesh=mesh,
        in_specs=(mesh_field, tap, tap, mesh_field, mesh_field, mesh_field, mesh_field, P(), block, block, block),
        out_specs=(mesh_field, block),
        check_vma=False,
    )
```

```python
import functools

import jax
import jax.numpy as jnp
from jax import lax
from jax.experimental import pallas as pl
from jax.experimental.pallas import tpu as pltpu
from jax.sharding import PartitionSpec as P

MESH = pl.DeviceIdType.MESH
F32 = jnp.float32
SWEEPS = 16
STEPS = 4
MATERIALS = 4
HALO = 20
PITCH = 24
TOP = 24
V = 13
W = 9
SRC, PAD, GXP, GYP, LEAK = range(5)
DIRS = ((-1, 0), (1, 0), (0, -1), (0, 1), (-1, -1), (-1, 1), (1, -1), (1, 1))


def iota(shape, dim):
    return lax.broadcasted_iota(jnp.int32, shape, dim)


def roll(x, shift, axis):
    return pltpu.roll(x, shift % x.shape[axis], axis)


def harmonic(a, b):
    total = a + b
    r = pl.reciprocal(total, approx=True)
    r = r * (2.0 - total * r)
    r = r * (2.0 - total * r)
    return 2.0 * a * b * r


def inverse_root(x):
    r = lax.rsqrt(x)
    return r * (1.5 - 0.5 * x * r * r)


def next_row(x):
    return jnp.concatenate([x[1:], roll(x[:1], -1, 1)], 0)


def last_row(x):
    return jnp.concatenate([roll(x[-1:], 1, 1), x[:-1]], 0)


def kernel(
    sizes,
    tidx_hbm, tcur_hbm, dens_hbm, pad_hbm, row_hbm, col_hbm, mat_hbm, rates_hbm, theta_hbm, kappa_hbm, invc_hbm,
    drop_out, temp_out,
    tidx, tcur, mat, rates, ext, row_send, row_recv, col_send, xr, yr, coef, raw, ub, nat, unat,
    field, trow_send, trow, tcol_send, tx, ty, edge, heat_send, heat,
    temp, east, west, aligned, cap, lx, ly, lw, lz, snat, stemp, scap, slx, sly, slz, sground, sheat, mix, begin, onat,
    isem, ssem, rsem, tssem, trsem, pssem, prsem,
):
    nx, ny, nz = sizes
    gx, gy, gz = lax.axis_index("gx"), lax.axis_index("gy"), lax.axis_index("gz")
    tiers, rows, cols = drop_out.shape
    layers = temp_out.shape[0]
    nc = ny * nz
    c = gy * nz + gz

    loads = [pltpu.make_async_copy(tidx_hbm, tidx, isem.at[0]), pltpu.make_async_copy(tcur_hbm, tcur, isem.at[1])]
    for a, ref in enumerate((dens_hbm, pad_hbm, row_hbm, col_hbm)):
        for tile in range(2):
            loads.append(pltpu.make_async_copy(
                ref.at[:, :, pl.ds(tile * 128, 128)], ext.at[a, :, tile, pl.ds(TOP, rows)], isem.at[len(loads)]
            ))
    loads.append(pltpu.make_async_copy(mat_hbm, mat, isem.at[len(loads)]))
    loads.append(pltpu.make_async_copy(rates_hbm, rates, isem.at[len(loads)]))
    heat_loads = [
        pltpu.make_async_copy(ref, field.at[a, :, pl.ds(8, rows)], isem.at[len(loads) + a])
        for a, ref in enumerate((theta_hbm, kappa_hbm, invc_hbm))
    ]
    for load in loads + heat_loads:
        load.start()

    def mesh_to(d):
        dx, dy = DIRS[d]
        return (lax.rem(gx + dx + nx, nx), lax.rem(gy + dy + ny, ny), gz)

    def heat_to(d):
        dx, dy = DIRS[d]
        there = lax.rem(c + dy + nc, nc)
        return (lax.rem(gx + dx + nx, nx), there // nz, lax.rem(there, nz))

    partner = (gx, gy, 1 - gz)

    barrier = pltpu.get_barrier_semaphore()
    for d in range(8):
        pl.semaphore_signal(barrier, inc=1, device_id=mesh_to(d), device_id_type=MESH)
    for d in range(2, 8):
        pl.semaphore_signal(barrier, inc=1, device_id=heat_to(d), device_id_type=MESH)

    def mesh_copy(d, t):
        top, bottom = pl.ds(0, TOP), pl.ds(rows - TOP, TOP)
        if d < 2:
            src, dst = row_send.at[d, t], row_recv.at[d, t]
        elif d == 2:
            src, dst = col_send.at[0, t], xr.at[t, pl.ds(TOP, rows)]
        elif d == 3:
            src, dst = col_send.at[1, t], yr.at[t, pl.ds(TOP, rows)]
        elif d == 4:
            src, dst = col_send.at[0, t, top], xr.at[t, pl.ds(TOP + rows, TOP)]
        elif d == 5:
            src, dst = col_send.at[1, t, top], yr.at[t, pl.ds(TOP + rows, TOP)]
        elif d == 6:
            src, dst = col_send.at[0, t, bottom], xr.at[t, pl.ds(0, TOP)]
        else:
            src, dst = col_send.at[1, t, bottom], yr.at[t, pl.ds(0, TOP)]
        return pltpu.make_async_remote_copy(
            src_ref=src, dst_ref=dst, send_sem=ssem.at[d, t], recv_sem=rsem.at[d, t],
            device_id=mesh_to(d), device_id_type=MESH,
        )

    def heat_copy(d):
        top, bottom = pl.ds(0, 8), pl.ds(rows - 8, 8)
        if d < 2:
            src, dst = trow_send.at[d], trow.at[d]
        elif d == 2:
            src, dst = tcol_send.at[0], tx.at[:, pl.ds(8, rows)]
        elif d == 3:
            src, dst = tcol_send.at[1], ty.at[:, pl.ds(8, rows)]
        elif d == 4:
            src, dst = tcol_send.at[0, :, top], tx.at[:, pl.ds(8 + rows, 8)]
        elif d == 5:
            src, dst = tcol_send.at[1, :, top], ty.at[:, pl.ds(8 + rows, 8)]
        elif d == 6:
            src, dst = tcol_send.at[0, :, bottom], tx.at[:, pl.ds(0, 8)]
        else:
            src, dst = tcol_send.at[1, :, bottom], ty.at[:, pl.ds(0, 8)]
        return pltpu.make_async_remote_copy(
            src_ref=src, dst_ref=dst, send_sem=tssem.at[d], recv_sem=trsem.at[d],
            device_id=heat_to(d), device_id_type=MESH,
        )

    def power_copy(t, z):
        return pltpu.make_async_remote_copy(
            src_ref=heat_send.at[t], dst_ref=heat.at[z * tiers + t], send_sem=pssem.at[t], recv_sem=prsem.at[t],
            device_id=partner, device_id_type=MESH,
        )

    def prepare(t):
        idx, cur = tidx[t], tcur[t]
        main = pl.ds(TOP, rows)
        lane = iota((rows, 128), 1)
        end_row = (iota((rows, 128), 0) == rows - 1) & (gx == nx - 1)
        end_col = (lane == 127) & (gy == ny - 1)
        edges = []
        for tile in range(2):
            spot = idx[tile : tile + 1]
            at_row = jnp.where(iota((rows, 128), 0) == (spot >> 7), cur[tile : tile + 1], 0.0)
            at_col = jnp.where(iota((128, 128), 0) == (spot & 127), 1.0, 0.0)
            taps = lax.dot_general(
                at_row, at_col, (((1,), (1,)), ((), ())),
                precision=lax.Precision.HIGHEST, preferred_element_type=F32,
            )
            source = ext[SRC, t, tile, main, :] + taps
            pad = ext[PAD, t, tile, main, :]
            gxp = jnp.where(end_row, 0.0, ext[GXP, t, tile, main, :])
            gyp = ext[GYP, t, tile, main, :]
            if tile == 1:
                gyp = jnp.where(end_col, 0.0, gyp)
            kinds = mat[t, :, tile * 128 : tile * 128 + 128]
            leak = jnp.zeros((rows, 128), F32)
            for kind in range(MATERIALS):
                leak = jnp.where(kinds == kind, rates[kind], leak)
            ext[SRC, t, tile, main, :] = source
            ext[GXP, t, tile, main, :] = gxp
            ext[GYP, t, tile, main, :] = gyp
            ext[LEAK, t, tile, main, :] = leak
            packed = jnp.zeros((rows, 128), F32)
            part = pl.ds(tile * 128, 128)
            for a, values in enumerate((source, pad, gxp, gyp, leak)):
                size = HALO if a < LEAK else 4
                at = a * HALO if a < LEAK else LEAK * HALO
                row_send[0, t, at : at + size, part] = values[:size]
                row_send[1, t, at : at + size, part] = values[rows - size :]
                mine = (lane >= a * PITCH) & (lane < a * PITCH + size)
                packed = jnp.where(mine, roll(values, a * PITCH + (size if tile else 0), 1), packed)
            row_send[0, t, 84:88, part] = jnp.zeros((4, 128), F32)
            row_send[1, t, 84:88, part] = jnp.zeros((4, 128), F32)
            col_send[tile, t] = packed

    def first_tiers(t, carry):
        prepare(t)

        @pl.when(t == 0)
        def _():
            pl.semaphore_wait(barrier, 14)

        for d in range(8):
            mesh_copy(d, t).start()
        return carry

    for load in loads:
        load.wait()
    lax.fori_loop(0, tiers, first_tiers, 0)

    lane_tall = iota((rows, 128), 1)
    sub = iota((16, 8, 128), 1)
    main = pl.ds(8, rows)
    for load in heat_loads:
        load.wait()
    for a in range(3):
        one, two = field[a, 0:16, 8:16, :], field[a, 16:32, 8:16, :]
        trow_send[0, a] = jnp.where(sub < 4, one, roll(two, 4, 1))
        one, two = field[a, 0:16, rows : rows + 8, :], field[a, 16:32, rows : rows + 8, :]
        trow_send[1, a] = jnp.where(sub < 4, roll(one, 4, 1), two)

    def gather(a, carry):
        low = high = jnp.zeros((rows, 128), F32)
        for l in range(16):
            mine = (lane_tall >> 3) == l
            low = jnp.where(mine, roll(field[a, l, main, :], 8 * l + 4, 1), low)
            high = jnp.where(mine, roll(field[a, l + 16, main, :], 8 * l + 4, 1), high)
        first = (lane_tall & 4) == 0
        tcol_send[0, a] = jnp.where(first, roll(high, -4, 1), low)
        tcol_send[1, a] = jnp.where(first, low, roll(high, 4, 1))
        edge[a, 0, main, :] = low
        edge[a, 1, main, :] = high
        return carry

    lax.fori_loop(0, 3, gather, 0)
    for d in range(8):
        heat_copy(d).start()

    lane_ext = iota((8, 384), 1)
    inside = (lane_ext < cols + HALO) | (lane_ext >= 384 - HALO)
    lane_rows = iota((rows + 2 * TOP, 128), 1)
    half = iota((8, 128), 1) < 64

    def halos(t, i):
        for d in range(8):
            mesh_copy(d, t).wait_recv()
        for a in range(5):
            size = HALO if a < LEAK else 4
            at = a * HALO if a < LEAK else LEAK * HALO
            for tile in range(2):
                part = pl.ds(tile * 128, 128)
                ext[a, t, tile, 0:8, :] = jnp.zeros((8, 128), F32)
                ext[a, t, tile, TOP - size : TOP, :] = row_recv[1, t, at : at + size, part]
                ext[a, t, tile, TOP + rows : TOP + rows + size, :] = row_recv[0, t, at : at + size, part]
                if a == LEAK:
                    ext[a, t, tile, 8 : TOP - size, :] = jnp.zeros((TOP - size - 8, 128), F32)
                    ext[a, t, tile, TOP + rows + size :, :] = jnp.zeros((TOP - size, 128), F32)
            ext[a, t, 2] = jnp.where(
                lane_rows < 64, roll(xr[t], -a * PITCH, 1), roll(yr[t], 128 - size - a * PITCH, 1)
            )

        def fetch(a, start):
            return jnp.concatenate([ext[a, t, tile, pl.ds(start, 8, stride=V), :] for tile in range(3)], 1)

        gxm = fetch(GXP, TOP - HALO - 1)
        for v in range(V):
            src, pd, gxp, gyp, leak = [fetch(a, TOP - HALO + v) for a in range(5)]
            r = jnp.where(inside, inverse_root(pd + gxp + gxm + gyp + roll(gyp, 1, 1)), 0.0)
            gxm = gxp
            for j, x in enumerate((pd, gxp, gyp, leak, r)):
                raw[i, j, v] = x
            coef[i, 0, v] = src * r
            coef[i, 2, v] = gyp * r * roll(r, -1, 1)
        for v in range(V):
            after = raw[i, 4, v + 1] if v < V - 1 else roll(raw[i, 4, 0], -1, 0)
            coef[i, 1, v] = raw[i, 1, v] * raw[i, 4, v] * after
        coef[i, 1, V] = roll(coef[i, 1, V - 1], 1, 0)

    def sweep(source_of, i, out):
        here = source_of(0)
        before, link_before = roll(source_of(V - 1), 1, 0), coef[i, 1, V]
        for v in range(V):
            after = source_of(v + 1) if v < V - 1 else roll(source_of(0), -1, 0)
            link, side = coef[i, 1, v], coef[i, 2, v]
            flow = link * after + link_before * before
            flow = flow + (side * roll(here, -1, 1) + roll(side * here, 1, 1))
            ub[i, out, v] = coef[i, 0, v] + flow
            before, here, link_before = here, after, link

    def power_of(t, i):
        here = first = ub[i, 0, 0] * raw[i, 4, 0]
        for v in range(V):
            after = ub[i, 0, v + 1] * raw[i, 4, v + 1] if v < V - 1 else roll(first, -1, 0)
            across, along = after - here, roll(here, -1, 1) - here
            power = raw[i, 0, v] * here * here + raw[i, 1, v] * across * across + raw[i, 2, v] * along * along
            power = power + raw[i, 3, v] * jnp.exp(-here)
            at = pl.ds(TOP - HALO + v, 8, stride=V)
            for tile in range(3):
                nat[i, tile, at, :] = power[:, tile * 128 : tile * 128 + 128]
                if tile < 2:
                    unat[i, tile, at, :] = here[:, tile * 128 : tile * 128 + 128]
            here = after

        for v in range(W):
            at = pl.ds(TOP - 4 + v, 8, stride=W)
            for z, into in ((1 - gz, heat_send.at[t]), (gz, heat.at[gz * tiers + t])):
                into[0, v] = nat[i, z, at, :]
                into[1, v] = jnp.where(half, nat[i, 1 + z, at, :], nat[i, 2 - 2 * z, at, :])
        power_copy(t, gz).start()
        for tile in range(2):
            drop_out[t, :, tile * 128 : tile * 128 + 128] = unat[i, tile, TOP : TOP + rows, :]

    def pair(p, carry):
        def each(work):
            lax.fori_loop(0, 2, lambda i, held: (work(2 * p + i, i), held)[1], 0)

        each(halos)
        for i in range(2):
            sweep(lambda v: coef[i, 0, v], i, 0)

        def two_sweeps(count, held):
            for here in range(2):
                for i in range(2):
                    sweep(lambda v: ub[i, here, v], i, 1 - here)
            return held

        lax.fori_loop(0, (SWEEPS - 2) // 2, two_sweeps, 0)
        each(power_of)
        return carry

    lax.fori_loop(0, tiers // 2, pair, 0)

    for d in range(8):
        heat_copy(d).wait_recv()
    lane8 = iota((8, 128), 1)
    lane_tall = iota((rows + 16, 128), 1)
    first = (lane_tall & 4) == 0

    def assemble(a, carry):
        above, below = trow[1, a], trow[0, a]
        field[a, 0:16, 0:8, :] = roll(above, 4, 1)
        field[a, 16:32, 0:8, :] = above
        field[a, 0:16, 8 + rows : 16 + rows, :] = below
        field[a, 16:32, 8 + rows : 16 + rows, :] = roll(below, 4, 1)
        up = down = jnp.zeros((8, 128), F32)
        for l in range(16):
            mine = (lane8 >> 3) == l
            up = jnp.where(mine, roll(above[l], 8 * l + 4, 1), up)
            down = jnp.where(mine, roll(below[l], 8 * l + 4, 1), down)
        edge[a, 0, 0:8, :] = roll(up, 4, 0)
        edge[a, 1, 0:8, :] = up
        edge[a, 0, 8 + rows : 16 + rows, :] = down
        edge[a, 1, 8 + rows : 16 + rows, :] = roll(down, 4, 0)
        x, y, low, high = tx[a], ty[a], edge[a, 0], edge[a, 1]
        snat[a, 0] = jnp.where(first, y, low)
        snat[a, 1] = jnp.where(first, low, x)
        snat[a, 2] = jnp.where(first, roll(y, -4, 1), high)
        snat[a, 3] = jnp.where(first, high, roll(x, 4, 1))
        return carry

    lax.fori_loop(0, 3, assemble, 0)

    shape = (W, 8, 128)
    row_of = iota(shape, 1) * W + iota(shape, 0) - 4
    lane = iota(shape, 2)
    no_row = ((row_of == rows - 1) & (gx == nx - 1)) | ((row_of == -1) & (gx == 0))
    no_col = (lane == 127) & (c == nc - 1)

    def strided(ref):
        return jnp.stack([ref[pl.ds(4 + v, 8, stride=W), :] for v in range(W)])

    def upper(low, high):
        return jnp.where(lane < 120, roll(low, -8, 2), roll(high, -8, 2)), roll(high, -8, 2)

    def align(x, layer):
        return pltpu.roll(x, lax.rem(252 - 8 * lax.rem(layer, 16), 128), 2)

    for side in range(2):
        k = [strided(snat.at[1, 2 * h + side]) for h in range(2)]
        over = upper(*k)
        no_edge = ((lane & 7) == 3) & (c == (nc - 1 if side else 0))
        sground[side] = k[0]
        for h in range(2):
            s = 2 * h + side
            stemp[s] = strided(snat.at[0, s])
            scap[s] = strided(snat.at[2, s])
            slx[s] = jnp.where(no_row, 0.0, harmonic(k[h], next_row(k[h])))
            sly[s] = jnp.where(no_edge, 0.0, harmonic(k[h], roll(k[h], -1, 2)))
            link = harmonic(k[h], over[h])
            slz[s] = jnp.where(lane < 120, link, 0.0) if h else link
            if side:
                mix[h] = jnp.where((lane & 7) == 3, sly[2 * h], k[h])
                begin[h] = jnp.where((lane & 7) == 3, stemp[2 * h], stemp[s])

    def beside(x, beyond):
        right = roll(jnp.where(lane == 0, beyond, x), -1, 2)
        left = roll(jnp.where(lane == 127, beyond, x), 1, 2)
        return right, left

    def links(layer, k):
        x = strided(field.at[0, layer])
        temp[0, layer] = x
        east[0, layer], west[0, layer] = beside(x, align(begin[layer // 16], layer))
        cap[layer] = strided(field.at[2, layer])
        over = strided(field.at[1, jnp.minimum(layer + 1, layers - 1)])
        beyond = align(mix[layer // 16], layer)
        right = harmonic(k, roll(jnp.where(lane == 0, beyond, k), -1, 2))
        right = jnp.where(no_col, 0.0, right)
        lx[layer] = jnp.where(no_row, 0.0, harmonic(k, next_row(k)))
        ly[layer] = right
        lw[layer] = roll(jnp.where(lane == 127, beyond, right), 1, 2)
        lz[layer + 1] = jnp.where(layer == layers - 1, 0.0, harmonic(k, over))
        return over

    ground = strided(field.at[1, 0])
    lz[0] = ground
    lax.fori_loop(0, layers, links, ground, unroll=4)

    for t in range(tiers):
        power_copy(t, 1 - gz).wait()

    for h in range(2):
        left = right = jnp.zeros(shape, F32)
        for t in range(4):
            inner, outer = heat[h * 4 + t, 0], heat[h * 4 + t, 1]
            mine = (lane >> 3) == 4 * t
            left = jnp.where(mine, roll(jnp.where(lane < 64, inner, outer), 32 * t + 4, 2), left)
            right = jnp.where(mine, roll(jnp.where(lane < 64, outer, inner), 32 * t + 4, 2), right)
        sheat[2 * h] = left
        sheat[2 * h + 1] = right

    def strips():
        for side in range(2):
            old = [stemp[side], stemp[2 + side]]
            over = upper(*old)
            rise = [slz[2 * h + side] * (over[h] - old[h]) for h in range(2)]
            under = (
                jnp.where(lane < 8, sground[side] * old[0], roll(rise[0], 8, 2)),
                jnp.where(lane < 8, roll(rise[0], 8, 2), roll(rise[1], 8, 2)),
            )
            for h in range(2):
                s = 2 * h + side
                here = old[h]
                fx = slx[s] * (next_row(here) - here)
                fy = sly[s] * (roll(here, -1, 2) - here)
                flow = (fx - last_row(fx)) + (fy - roll(fy, 1, 2)) + (rise[h] - under[h]) + sheat[s]
                after = here + scap[s] * flow
                stemp[s] = after
                mix[h] = jnp.where((lane & 7) == 3, mix[h], after) if side else after

    def shift(layer, into):
        return beside(temp[into, layer], aligned[layer])

    for count in range(STEPS):
        now, then, more = count % 2, 1 - count % 2, count < STEPS - 1
        if more:
            strips()
        if count:
            for layer in range(layers - 4, layers):
                east[now, layer], west[now, layer] = shift(layer, now)

        def group(g, below, now=now, then=then, more=more):
            base = 4 * g
            if more:
                prior = 4 * jnp.maximum(g - 1, 0)
                shifted = [shift(prior + part, then) for part in range(4)]
            fresh = []
            here = temp[now, base]
            for part in range(4):
                layer = base + part
                over = temp[now, layer + 1 if part < 3 else jnp.minimum(layer + 1, layers - 1)]
                fx = lx[layer] * (next_row(here) - here)
                fz = lz[layer + 1] * (over - here)
                flow = ly[layer] * (east[now, layer] - here) + lw[layer] * (west[now, layer] - here)
                flow = flow + (fx - last_row(fx)) + (fz - below)
                if part == 0:
                    flow = flow + heat[g, 0]
                fresh.append(here + cap[layer] * flow)
                here, below = over, fz
            for part in range(4):
                temp[then, base + part] = fresh[part]
                if more:
                    east[then, prior + part], west[then, prior + part] = shifted[part]
                    aligned[base + part] = align(mix[g // 4], base + part)
            return below

        lax.fori_loop(0, layers // 4, group, lz[0] * temp[now, 0])

    def result(layer, carry):
        for v in range(W):
            onat[layer, pl.ds(4 + v, 8, stride=W), :] = temp[STEPS % 2, layer, v]
        temp_out[layer] = onat[layer, pl.ds(8, rows), :]
        return carry

    lax.fori_loop(0, layers, result, 0, unroll=4)

    def finish(t, carry):
        for d in range(8):
            mesh_copy(d, t).wait_send()
        return carry

    lax.fori_loop(0, tiers, finish, 0)
    for d in range(8):
        heat_copy(d).wait_send()


def shards(sizes, density, tap_index, tap_current, pad_cond, row_cond, col_cond, material, leak_rates, theta, kappa, invc):
    tiers, rows, cols = density.shape
    layers = theta.shape[0]
    vmem, hbm = pl.BlockSpec(memory_space=pltpu.VMEM), pl.BlockSpec(memory_space=pltpu.HBM)
    tall, high = rows + 2 * TOP, rows + 16
    dma = pltpu.SemaphoreType.DMA
    taps = tap_index.shape[-1]
    scratch = [
        (5, tiers, 3, tall, 128),
        (2, tiers, 88, cols), (2, tiers, 88, cols), (2, tiers, rows, 128),
        (tiers, tall, 128), (tiers, tall, 128),
        (2, 3, V + 1, 8, 384), (2, 5, V, 8, 384), (2, 2, V, 8, 384),
        (2, 3, tall, 128), (2, 2, tall, 128),
        (3, layers, high, 128),
        (2, 3, 16, 8, 128), (2, 3, 16, 8, 128),
        (2, 3, rows, 128), (3, high, 128), (3, high, 128), (3, 2, high, 128),
        (tiers, 2, W, 8, 128), (2 * tiers, 2, W, 8, 128),
        (2, layers, W, 8, 128), (2, layers, W, 8, 128), (2, layers, W, 8, 128),
        (layers, W, 8, 128), (layers, W, 8, 128),
        (layers, W, 8, 128), (layers, W, 8, 128), (layers, W, 8, 128), (layers + 1, W, 8, 128),
        (3, 4, high, 128),
        (4, W, 8, 128), (4, W, 8, 128), (4, W, 8, 128), (4, W, 8, 128), (4, W, 8, 128),
        (2, W, 8, 128), (4, W, 8, 128), (2, W, 8, 128), (2, W, 8, 128),
        (layers, high, 128),
    ]
    return pl.pallas_call(
        functools.partial(kernel, sizes),
        out_shape=(jax.ShapeDtypeStruct((tiers, rows, cols), F32), jax.ShapeDtypeStruct(theta.shape, F32)),
        in_specs=[hbm] * 11,
        out_specs=(vmem, vmem),
        scratch_shapes=[
            pltpu.VMEM((tiers, 2, taps), jnp.int32),
            pltpu.VMEM((tiers, 2, taps), F32),
            pltpu.VMEM((tiers, rows, cols), jnp.int32),
            pltpu.SMEM((MATERIALS,), F32),
            *[pltpu.VMEM(size, F32) for size in scratch],
            dma((15,)), dma((8, tiers)), dma((8, tiers)), dma((8,)), dma((8,)), dma((tiers,)), dma((tiers,)),
        ],
        compiler_params=pltpu.CompilerParams(
            collective_id=0, has_side_effects=True, vmem_limit_bytes=34 * 2**20
        ),
        name="electrothermal",
    )(
        *[pltpu.with_memory_space_constraint(x, pltpu.HBM) for x in (
            tap_index.reshape(tiers, 2, taps), tap_current.reshape(tiers, 2, taps), density, pad_cond, row_cond,
            col_cond, material, leak_rates, theta, kappa, invc,
        )],
    )


def solution(mesh):
    sizes = tuple(mesh.shape[name] for name in ("gx", "gy", "gz"))
    mesh_field = P("gz", "gx", "gy")
    tap = P("gz", "gx", "gy", None)
    block = P(None, "gx", ("gy", "gz"))
    return jax.shard_map(
        functools.partial(shards, sizes),
        mesh=mesh,
        in_specs=(mesh_field, tap, tap, mesh_field, mesh_field, mesh_field, mesh_field, P(), block, block, block),
        out_specs=(mesh_field, block),
        check_vma=False,
    )
```

```python
import functools

import jax
import jax.numpy as jnp
from jax import lax
from jax.experimental import pallas as pl
from jax.experimental.pallas import tpu as pltpu
from jax.sharding import PartitionSpec as P

MESH = pl.DeviceIdType.MESH
F32 = jnp.float32
SWEEPS = 16
STEPS = 4
MATERIALS = 4
HALO = 20
DEEP = 19
PITCH = 24
TOP = 24
V = 13
W = 9
SRC, PAD, GXP, GYP, LEAK = range(5)
DIRS = ((-1, 0), (1, 0), (0, -1), (0, 1), (-1, -1), (-1, 1), (1, -1), (1, 1))


def iota(shape, dim):
    return lax.broadcasted_iota(jnp.int32, shape, dim)


def roll(x, shift, axis):
    return pltpu.roll(x, shift % x.shape[axis], axis)


def harmonic(a, b):
    total = a + b
    r = pl.reciprocal(total, approx=True)
    r = r * (2.0 - total * r)
    r = r * (2.0 - total * r)
    return 2.0 * a * b * r


def inverse_root(x):
    r = lax.rsqrt(x)
    return r * (1.5 - 0.5 * x * r * r)


def next_row(x):
    return jnp.concatenate([x[1:], roll(x[:1], -1, 1)], 0)


def last_row(x):
    return jnp.concatenate([roll(x[-1:], 1, 1), x[:-1]], 0)


def kernel(
    sizes,
    tidx_hbm, tcur_hbm, dens_hbm, pad_hbm, row_hbm, col_hbm, mat_hbm, rates_hbm, theta_hbm, kappa_hbm, invc_hbm,
    drop_out, temp_out,
    tidx, tcur, mat, rates, ext, row_send, row_recv, col_send, xr, yr, coef, raw, ub, nat, unat,
    field, trow_send, trow, tcol_send, tx, ty, edge, heat_send, heat,
    temp_a, temp_b, east_a, east_b, west_a, west_b, aligned, cap, lx, ly, lw, lz, snat, stemp, scap, slx, sly, slz, sground, sheat, mix, begin, onat,
    isem, ssem, rsem, tssem, trsem, pssem, prsem,
):
    nx, ny, nz = sizes
    gx, gy, gz = lax.axis_index("gx"), lax.axis_index("gy"), lax.axis_index("gz")
    tiers, rows, cols = drop_out.shape
    layers = temp_out.shape[0]
    nc = ny * nz
    c = gy * nz + gz

    loads = [pltpu.make_async_copy(tidx_hbm, tidx, isem.at[0]), pltpu.make_async_copy(tcur_hbm, tcur, isem.at[1])]
    for a, ref in enumerate((dens_hbm, pad_hbm, row_hbm, col_hbm)):
        for tile in range(2):
            loads.append(pltpu.make_async_copy(
                ref.at[:, :, pl.ds(tile * 128, 128)], ext.at[a, :, tile, pl.ds(TOP, rows)], isem.at[len(loads)]
            ))
    loads.append(pltpu.make_async_copy(mat_hbm, mat, isem.at[len(loads)]))
    loads.append(pltpu.make_async_copy(rates_hbm, rates, isem.at[len(loads)]))
    heat_loads = [
        pltpu.make_async_copy(ref, field.at[a, :, pl.ds(8, rows)], isem.at[len(loads) + a])
        for a, ref in enumerate((theta_hbm, kappa_hbm, invc_hbm))
    ]
    for load in loads:
        load.start()

    def mesh_to(d):
        dx, dy = DIRS[d]
        return (lax.rem(gx + dx + nx, nx), lax.rem(gy + dy + ny, ny), gz)

    def heat_to(d):
        dx, dy = DIRS[d]
        there = lax.rem(c + dy + nc, nc)
        return (lax.rem(gx + dx + nx, nx), there // nz, lax.rem(there, nz))

    partner = (gx, gy, 1 - gz)

    barrier = pltpu.get_barrier_semaphore()
    for d in range(8):
        pl.semaphore_signal(barrier, inc=1, device_id=mesh_to(d), device_id_type=MESH)
    for d in range(2, 8):
        pl.semaphore_signal(barrier, inc=1, device_id=heat_to(d), device_id_type=MESH)

    def mesh_copy(d, p):
        t = pl.ds(2 * p, 2)
        top, bottom = pl.ds(0, TOP), pl.ds(rows - TOP, TOP)
        if d < 2:
            src, dst = row_send.at[d, t], row_recv.at[d, t]
        elif d == 2:
            src, dst = col_send.at[0, t], xr.at[t, pl.ds(TOP, rows)]
        elif d == 3:
            src, dst = col_send.at[1, t], yr.at[t, pl.ds(TOP, rows)]
        elif d == 4:
            src, dst = col_send.at[0, t, top], xr.at[t, pl.ds(TOP + rows, TOP)]
        elif d == 5:
            src, dst = col_send.at[1, t, top], yr.at[t, pl.ds(TOP + rows, TOP)]
        elif d == 6:
            src, dst = col_send.at[0, t, bottom], xr.at[t, pl.ds(0, TOP)]
        else:
            src, dst = col_send.at[1, t, bottom], yr.at[t, pl.ds(0, TOP)]
        return pltpu.make_async_remote_copy(
            src_ref=src, dst_ref=dst, send_sem=ssem.at[d, p], recv_sem=rsem.at[d, p],
            device_id=mesh_to(d), device_id_type=MESH,
        )

    def heat_copy(d):
        top, bottom = pl.ds(0, 8), pl.ds(rows - 8, 8)
        if d < 2:
            src, dst = trow_send.at[d], trow.at[d]
        elif d == 2:
            src, dst = tcol_send.at[0], tx.at[:, pl.ds(8, rows)]
        elif d == 3:
            src, dst = tcol_send.at[1], ty.at[:, pl.ds(8, rows)]
        elif d == 4:
            src, dst = tcol_send.at[0, :, top], tx.at[:, pl.ds(8 + rows, 8)]
        elif d == 5:
            src, dst = tcol_send.at[1, :, top], ty.at[:, pl.ds(8 + rows, 8)]
        elif d == 6:
            src, dst = tcol_send.at[0, :, bottom], tx.at[:, pl.ds(0, 8)]
        else:
            src, dst = tcol_send.at[1, :, bottom], ty.at[:, pl.ds(0, 8)]
        return pltpu.make_async_remote_copy(
            src_ref=src, dst_ref=dst, send_sem=tssem.at[d], recv_sem=trsem.at[d],
            device_id=heat_to(d), device_id_type=MESH,
        )

    def power_copy(t, z):
        return pltpu.make_async_remote_copy(
            src_ref=heat_send.at[t], dst_ref=heat.at[z * tiers + t], send_sem=pssem.at[t], recv_sem=prsem.at[t],
            device_id=partner, device_id_type=MESH,
        )

    def prepare(t):
        idx, cur = tidx[t], tcur[t]
        main = pl.ds(TOP, rows)
        lane = iota((rows, 128), 1)
        end_row = (iota((rows, 128), 0) == rows - 1) & (gx == nx - 1)
        end_col = (lane == 127) & (gy == ny - 1)
        edges = []
        for tile in range(2):
            spot = idx[tile : tile + 1]
            at_row = jnp.where(iota((rows, 128), 0) == (spot >> 7), cur[tile : tile + 1], 0.0)
            at_col = jnp.where(iota((128, 128), 0) == (spot & 127), 1.0, 0.0)
            taps = lax.dot_general(
                at_row, at_col, (((1,), (1,)), ((), ())),
                precision=lax.Precision.HIGHEST, preferred_element_type=F32,
            )
            source = ext[SRC, t, tile, main, :] + taps
            pad = ext[PAD, t, tile, main, :]
            gxp = jnp.where(end_row, 0.0, ext[GXP, t, tile, main, :])
            gyp = ext[GYP, t, tile, main, :]
            if tile == 1:
                gyp = jnp.where(end_col, 0.0, gyp)
            kinds = mat[t, :, tile * 128 : tile * 128 + 128]
            leak = jnp.zeros((rows, 128), F32)
            for kind in range(MATERIALS):
                leak = jnp.where(kinds == kind, rates[kind], leak)
            ext[SRC, t, tile, main, :] = source
            ext[GXP, t, tile, main, :] = gxp
            ext[GYP, t, tile, main, :] = gyp
            ext[LEAK, t, tile, main, :] = leak
            packed = jnp.zeros((rows, 128), F32)
            part = pl.ds(tile * 128, 128)
            for a, values in enumerate((source, pad, gxp, gyp, leak)):
                deep = DEEP if a < LEAK else 3
                at = a * DEEP
                row_send[0, t, at : at + deep, part] = values[:deep]
                row_send[1, t, at : at + deep, part] = values[rows - deep :]
                size = HALO if a < LEAK else 4
                mine = (lane >= a * PITCH) & (lane < a * PITCH + size)
                packed = jnp.where(mine, roll(values, a * PITCH + (size if tile else 0), 1), packed)
            row_send[0, t, 79:80, part] = jnp.zeros((1, 128), F32)
            row_send[1, t, 79:80, part] = jnp.zeros((1, 128), F32)
            col_send[tile, t] = packed

    def first_tiers(t, carry):
        prepare(t)

        @pl.when(t == 1)
        def _():
            pl.semaphore_wait(barrier, 14)

        @pl.when(lax.rem(t, 2) == 1)
        def _():
            for d in (4, 5, 6, 7, 0, 1, 2, 3):
                mesh_copy(d, t // 2).start()

        return carry

    for load in loads:
        load.wait()
    for load in heat_loads:
        load.start()
    lax.fori_loop(0, tiers, first_tiers, 0)

    lane_tall = iota((rows, 128), 1)
    sub = iota((16, 8, 128), 1)
    main = pl.ds(8, rows)
    for load in heat_loads:
        load.wait()
    for a in range(3):
        one, two = field[a, 0:16, 8:16, :], field[a, 16:32, 8:16, :]
        trow_send[0, a] = jnp.where(sub < 4, one, roll(two, 4, 1))
        one, two = field[a, 0:16, rows : rows + 8, :], field[a, 16:32, rows : rows + 8, :]
        trow_send[1, a] = jnp.where(sub < 4, roll(one, 4, 1), two)

    def gather(a, carry):
        low = high = jnp.zeros((rows, 128), F32)
        for l in range(16):
            mine = (lane_tall >> 3) == l
            low = jnp.where(mine, roll(field[a, l, main, :], 8 * l + 4, 1), low)
            high = jnp.where(mine, roll(field[a, l + 16, main, :], 8 * l + 4, 1), high)
        first = (lane_tall & 4) == 0
        tcol_send[0, a] = jnp.where(first, roll(high, -4, 1), low)
        tcol_send[1, a] = jnp.where(first, low, roll(high, 4, 1))
        edge[a, 0, main, :] = low
        edge[a, 1, main, :] = high
        return carry

    lax.fori_loop(0, 3, gather, 0)

    for d in range(8):
        heat_copy(d).start()

    lane_ext = iota((8, 384), 1)
    inside = (lane_ext < cols + HALO) | (lane_ext >= 384 - HALO)
    lane_rows = iota((rows + 2 * TOP, 128), 1)
    lane_one = iota((8, 128), 1)
    half = lane_one < 64

    def halos(t, i):
        for a in range(5):
            size, deep = (HALO, DEEP) if a < LEAK else (4, 3)
            at = a * DEEP
            outside = jnp.full((TOP, 128), 1.0 if a == PAD else 0.0, F32)
            for tile in range(2):
                part = pl.ds(tile * 128, 128)
                ext[a, t, tile, 0:TOP, :] = outside
                ext[a, t, tile, TOP - deep : TOP, :] = row_recv[1, t, at : at + deep, part]
                ext[a, t, tile, TOP + rows :, :] = outside
                ext[a, t, tile, TOP + rows : TOP + rows + deep, :] = row_recv[0, t, at : at + deep, part]
            ext[a, t, 2] = jnp.where(
                lane_rows < 64, roll(xr[t], -a * PITCH, 1), roll(yr[t], 128 - size - a * PITCH, 1)
            )

        def fetch(a, start):
            return jnp.concatenate([ext[a, t, tile, pl.ds(start, 8, stride=V), :] for tile in range(3)], 1)

        gxm = fetch(GXP, TOP - HALO - 1)
        for v in range(V):
            src, pd, gxp, gyp, leak = [fetch(a, TOP - HALO + v) for a in range(5)]
            r = jnp.where(inside, inverse_root(pd + gxp + gxm + gyp + roll(gyp, 1, 1)), 0.0)
            gxm = gxp
            for j, x in enumerate((pd, gxp, gyp, leak, r)):
                raw[i, j, v] = x
            coef[i, 0, v] = src * r
            coef[i, 2, v] = gyp * r * roll(r, -1, 1)
        for v in range(V):
            after = raw[i, 4, v + 1] if v < V - 1 else roll(raw[i, 4, 0], -1, 0)
            coef[i, 1, v] = raw[i, 1, v] * raw[i, 4, v] * after
        coef[i, 1, V] = roll(coef[i, 1, V - 1], 1, 0)

    def sweep(source_of, i, out):
        here = source_of(0)
        before, link_before = roll(source_of(V - 1), 1, 0), coef[i, 1, V]
        for v in range(V):
            after = source_of(v + 1) if v < V - 1 else roll(source_of(0), -1, 0)
            link, side = coef[i, 1, v], coef[i, 2, v]
            flow = link * after + link_before * before
            flow = flow + (side * roll(here, -1, 1) + roll(side * here, 1, 1))
            ub[i, out, v] = coef[i, 0, v] + flow
            before, here, link_before = here, after, link

    def power_of(t, i):
        here = first = ub[i, 0, 0] * raw[i, 4, 0]
        for v in range(V):
            after = ub[i, 0, v + 1] * raw[i, 4, v + 1] if v < V - 1 else roll(first, -1, 0)
            across, along = after - here, roll(here, -1, 1) - here
            power = raw[i, 0, v] * here * here + raw[i, 1, v] * across * across + raw[i, 2, v] * along * along
            power = power + raw[i, 3, v] * jnp.exp(-here)
            at = pl.ds(TOP - HALO + v, 8, stride=V)
            for tile in range(3):
                nat[i, tile, at, :] = power[:, tile * 128 : tile * 128 + 128]
                if tile < 2:
                    unat[i, tile, at, :] = here[:, tile * 128 : tile * 128 + 128]
            here = after

        for z, into in ((1 - gz, heat_send.at[t]), (gz, heat.at[gz * tiers + t])):
            packed = jnp.zeros((8, 128), F32)
            for v in range(W):
                at = pl.ds(TOP - 4 + v, 8, stride=W)
                into[v] = nat[i, z, at, :]
                outer = jnp.where(half, nat[i, 1 + z, at, :], nat[i, 2 - 2 * z, at, :])
                packed = jnp.where((lane_one >> 3) == v, roll(outer, 8 * v + 4, 1), packed)
            into[W] = packed
        power_copy(t, gz).start()
        for tile in range(2):
            drop_out[t, :, tile * 128 : tile * 128 + 128] = unat[i, tile, TOP : TOP + rows, :]

    def pair(p, carry):
        def each(work):
            lax.fori_loop(0, 2, lambda i, held: (work(2 * p + i, i), held)[1], 0)

        for d in range(8):
            mesh_copy(d, p).wait_recv()
        each(halos)
        for i in range(2):
            sweep(lambda v: coef[i, 0, v], i, 0)

        def two_sweeps(count, held):
            for here in range(2):
                for i in range(2):
                    sweep(lambda v: ub[i, here, v], i, 1 - here)
            return held

        lax.fori_loop(0, (SWEEPS - 2) // 2, two_sweeps, 0)
        each(power_of)
        return carry

    lax.fori_loop(0, tiers // 2, pair, 0)

    for d in range(8):
        heat_copy(d).wait_recv()
    lane8 = iota((8, 128), 1)
    lane_tall = iota((rows + 16, 128), 1)
    first = (lane_tall & 4) == 0

    def assemble(a, carry):
        above, below = trow[1, a], trow[0, a]
        field[a, 0:16, 0:8, :] = roll(above, 4, 1)
        field[a, 16:32, 0:8, :] = above
        field[a, 0:16, 8 + rows : 16 + rows, :] = below
        field[a, 16:32, 8 + rows : 16 + rows, :] = roll(below, 4, 1)
        up = down = jnp.zeros((8, 128), F32)
        for l in range(16):
            mine = (lane8 >> 3) == l
            up = jnp.where(mine, roll(above[l], 8 * l + 4, 1), up)
            down = jnp.where(mine, roll(below[l], 8 * l + 4, 1), down)
        edge[a, 0, 0:8, :] = roll(up, 4, 0)
        edge[a, 1, 0:8, :] = up
        edge[a, 0, 8 + rows : 16 + rows, :] = down
        edge[a, 1, 8 + rows : 16 + rows, :] = roll(down, 4, 0)
        x, y, low, high = tx[a], ty[a], edge[a, 0], edge[a, 1]
        snat[a, 0] = jnp.where(first, y, low)
        snat[a, 1] = jnp.where(first, low, x)
        snat[a, 2] = jnp.where(first, roll(y, -4, 1), high)
        snat[a, 3] = jnp.where(first, high, roll(x, 4, 1))
        return carry

    lax.fori_loop(0, 3, assemble, 0)

    shape = (W, 8, 128)
    row_of = iota(shape, 1) * W + iota(shape, 0) - 4
    lane = iota(shape, 2)
    no_row = ((row_of == rows - 1) & (gx == nx - 1)) | ((row_of == -1) & (gx == 0))
    no_col = (lane == 127) & (c == nc - 1)

    def strided(ref):
        return jnp.stack([ref[pl.ds(4 + v, 8, stride=W), :] for v in range(W)])

    def upper(low, high):
        return jnp.where(lane < 120, roll(low, -8, 2), roll(high, -8, 2)), roll(high, -8, 2)

    def align(x, layer):
        return pltpu.roll(x, lax.rem(252 - 8 * lax.rem(layer, 16), 128), 2)

    for side in range(2):
        k = [strided(snat.at[1, 2 * h + side]) for h in range(2)]
        over = upper(*k)
        no_edge = ((lane & 7) == 3) & (c == (nc - 1 if side else 0))
        sground[side] = k[0]
        for h in range(2):
            s = 2 * h + side
            stemp[s] = strided(snat.at[0, s])
            scap[s] = strided(snat.at[2, s])
            slx[s] = jnp.where(no_row, 0.0, harmonic(k[h], next_row(k[h])))
            sly[s] = jnp.where(no_edge, 0.0, harmonic(k[h], roll(k[h], -1, 2)))
            link = harmonic(k[h], over[h])
            slz[s] = jnp.where(lane < 120, link, 0.0) if h else link
            if side:
                mix[h] = jnp.where((lane & 7) == 3, sly[2 * h], k[h])
                begin[h] = jnp.where((lane & 7) == 3, stemp[2 * h], stemp[s])

    def beside(x, beyond):
        right = roll(jnp.where(lane == 0, beyond, x), -1, 2)
        left = roll(jnp.where(lane == 127, beyond, x), 1, 2)
        return right, left

    def bring(layer, carry):
        aligned[layer] = align(begin[layer // 16], layer)
        east_b[layer] = align(mix[layer // 16], layer)
        return carry

    lax.fori_loop(0, layers, bring, 0, unroll=4)

    def links(layer, k):
        x = strided(field.at[0, layer])
        temp_a[layer] = x
        east_a[layer], west_a[layer] = beside(x, aligned[layer])
        cap[layer] = strided(field.at[2, layer])
        over = strided(field.at[1, jnp.minimum(layer + 1, layers - 1)])
        beyond = east_b[layer]
        right = harmonic(k, roll(jnp.where(lane == 0, beyond, k), -1, 2))
        right = jnp.where(no_col, 0.0, right)
        lx[layer] = jnp.where(no_row, 0.0, harmonic(k, next_row(k)))
        ly[layer] = right
        lw[layer] = roll(jnp.where(lane == 127, beyond, right), 1, 2)
        lz[layer + 1] = jnp.where(layer == layers - 1, 0.0, harmonic(k, over))
        return over

    ground = strided(field.at[1, 0])
    lz[0] = ground
    lax.fori_loop(0, layers, links, ground, unroll=4)

    for t in range(tiers):
        power_copy(t, 1 - gz).wait()

    for h in range(2):
        left = right = jnp.zeros(shape, F32)
        for t in range(4):
            inner, packed = heat[h * 4 + t, 0:W], heat[h * 4 + t, W]
            outer = jnp.stack([roll(packed, -8 * v - 4, 1) for v in range(W)])
            mine = (lane >> 3) == 4 * t
            left = jnp.where(mine, roll(jnp.where(lane < 64, inner, outer), 32 * t + 4, 2), left)
            right = jnp.where(mine, roll(jnp.where(lane < 64, outer, inner), 32 * t + 4, 2), right)
        sheat[2 * h] = left
        sheat[2 * h + 1] = right

    def strips():
        for side in range(2):
            old = [stemp[side], stemp[2 + side]]
            over = upper(*old)
            rise = [slz[2 * h + side] * (over[h] - old[h]) for h in range(2)]
            under = (
                jnp.where(lane < 8, sground[side] * old[0], roll(rise[0], 8, 2)),
                jnp.where(lane < 8, roll(rise[0], 8, 2), roll(rise[1], 8, 2)),
            )
            for h in range(2):
                s = 2 * h + side
                here = old[h]
                fx = slx[s] * (next_row(here) - here)
                fy = sly[s] * (roll(here, -1, 2) - here)
                flow = (fx - last_row(fx)) + (fy - roll(fy, 1, 2)) + (rise[h] - under[h]) + sheat[s]
                after = here + scap[s] * flow
                stemp[s] = after
                mix[h] = jnp.where((lane & 7) == 3, mix[h], after) if side else after

    def shift(layer, state):
        temp, east, west = state
        east[layer], west[layer] = beside(temp[layer], aligned[layer])

    states = ((temp_a, east_a, west_a), (temp_b, east_b, west_b))
    for count in range(STEPS):
        now, then, more = states[count % 2], states[1 - count % 2], count < STEPS - 1
        if more:
            strips()
        if count:
            for layer in range(layers - 4, layers):
                shift(layer, now)

        def group(g, below, now=now, then=then, more=more):
            temp, east, west = now
            base = 4 * g
            if more:
                for part in range(4):
                    shift(4 * jnp.maximum(g - 1, 0) + part, then)
            for part in range(4):
                layer = base + part
                over = layer + 1 if part < 3 else jnp.minimum(layer + 1, layers - 1)
                fx_last = roll(lx[layer, W - 1] * (roll(temp[layer, 0], -1, 0) - temp[layer, W - 1]), 1, 0)
                rise = []
                for v in range(W):
                    here = temp[layer, v]
                    after = temp[layer, v + 1] if v < W - 1 else roll(temp[layer, 0], -1, 0)
                    fx = lx[layer, v] * (after - here)
                    fz = lz[layer + 1, v] * (temp[over, v] - here)
                    flow = ly[layer, v] * (east[layer, v] - here) + lw[layer, v] * (west[layer, v] - here)
                    flow = flow + (fx - fx_last) + (fz - below[v])
                    if part == 0:
                        flow = flow + heat[g, v]
                    then[0][layer, v] = here + cap[layer, v] * flow
                    fx_last = fx
                    rise.append(fz)
                below = tuple(rise)
                if more:
                    aligned[layer] = align(mix[g // 4], layer)
            return below

        lax.fori_loop(0, layers // 4, group, tuple(lz[0, v] * now[0][0, v] for v in range(W)))

    def result(layer, carry):
        for v in range(W):
            onat[layer, pl.ds(4 + v, 8, stride=W), :] = states[STEPS % 2][0][layer, v]
        temp_out[layer] = onat[layer, pl.ds(8, rows), :]
        return carry

    lax.fori_loop(0, layers, result, 0, unroll=4)

    for d in range(8):
        heat_copy(d).wait_send()
    for p in range(tiers // 2):
        for d in range(8):
            mesh_copy(d, p).wait_send()


def shards(sizes, density, tap_index, tap_current, pad_cond, row_cond, col_cond, material, leak_rates, theta, kappa, invc):
    tiers, rows, cols = density.shape
    layers = theta.shape[0]
    vmem, hbm = pl.BlockSpec(memory_space=pltpu.VMEM), pl.BlockSpec(memory_space=pltpu.HBM)
    tall, high = rows + 2 * TOP, rows + 16
    dma = pltpu.SemaphoreType.DMA
    taps = tap_index.shape[-1]
    scratch = [
        (5, tiers, 3, tall, 128),
        (2, tiers, 80, cols), (2, tiers, 80, cols), (2, tiers, rows, 128),
        (tiers, tall, 128), (tiers, tall, 128),
        (2, 3, V + 1, 8, 384), (2, 5, V, 8, 384), (2, 2, V, 8, 384),
        (2, 3, tall, 128), (2, 2, tall, 128),
        (3, layers, high, 128),
        (2, 3, 16, 8, 128), (2, 3, 16, 8, 128),
        (2, 3, rows, 128), (3, high, 128), (3, high, 128), (3, 2, high, 128),
        (tiers, W + 1, 8, 128), (2 * tiers, W + 1, 8, 128),
        *[(layers, W, 8, 128)] * 6,
        (layers, W, 8, 128), (layers, W, 8, 128),
        (layers, W, 8, 128), (layers, W, 8, 128), (layers, W, 8, 128), (layers + 1, W, 8, 128),
        (3, 4, high, 128),
        (4, W, 8, 128), (4, W, 8, 128), (4, W, 8, 128), (4, W, 8, 128), (4, W, 8, 128),
        (2, W, 8, 128), (4, W, 8, 128), (2, W, 8, 128), (2, W, 8, 128),
        (layers, high, 128),
    ]
    return pl.pallas_call(
        functools.partial(kernel, sizes),
        out_shape=(jax.ShapeDtypeStruct((tiers, rows, cols), F32), jax.ShapeDtypeStruct(theta.shape, F32)),
        in_specs=[hbm] * 11,
        out_specs=(vmem, vmem),
        scratch_shapes=[
            pltpu.VMEM((tiers, 2, taps), jnp.int32),
            pltpu.VMEM((tiers, 2, taps), F32),
            pltpu.VMEM((tiers, rows, cols), jnp.int32),
            pltpu.SMEM((MATERIALS,), F32),
            *[pltpu.VMEM(size, F32) for size in scratch],
            dma((15,)), dma((8, tiers // 2)), dma((8, tiers // 2)), dma((8,)), dma((8,)), dma((tiers,)), dma((tiers,)),
        ],
        compiler_params=pltpu.CompilerParams(
            collective_id=0, has_side_effects=True, vmem_limit_bytes=34 * 2**20
        ),
        name="electrothermal",
    )(
        *[pltpu.with_memory_space_constraint(x, pltpu.HBM) for x in (
            tap_index.reshape(tiers, 2, taps), tap_current.reshape(tiers, 2, taps), density, pad_cond, row_cond,
            col_cond, material, leak_rates, theta, kappa, invc,
        )],
    )


def solution(mesh):
    sizes = tuple(mesh.shape[name] for name in ("gx", "gy", "gz"))
    mesh_field = P("gz", "gx", "gy")
    tap = P("gz", "gx", "gy", None)
    block = P(None, "gx", ("gy", "gz"))
    return jax.shard_map(
        functools.partial(shards, sizes),
        mesh=mesh,
        in_specs=(mesh_field, tap, tap, mesh_field, mesh_field, mesh_field, mesh_field, P(), block, block, block),
        out_specs=(mesh_field, block),
        check_vma=False,
    )
```

```python
import functools

import jax
import jax.numpy as jnp
from jax import lax
from jax.experimental import pallas as pl
from jax.experimental.pallas import tpu as pltpu
from jax.sharding import PartitionSpec as P

MESH = pl.DeviceIdType.MESH
F32 = jnp.float32
SWEEPS = 16
STEPS = 4
MATERIALS = 4
HALO = 20
DEEP = 19
PITCH = 24
TOP = 24
V = 13
W = 9
SRC, PAD, GXP, GYP, LEAK = range(5)
DIRS = ((-1, 0), (1, 0), (0, -1), (0, 1), (-1, -1), (-1, 1), (1, -1), (1, 1))


def iota(shape, dim):
    return lax.broadcasted_iota(jnp.int32, shape, dim)


def roll(x, shift, axis):
    return pltpu.roll(x, shift % x.shape[axis], axis)


def harmonic(a, b):
    total = a + b
    r = pl.reciprocal(total, approx=True)
    r = r * (2.0 - total * r)
    r = r * (2.0 - total * r)
    return 2.0 * a * b * r


def inverse_root(x):
    r = lax.rsqrt(x)
    return r * (1.5 - 0.5 * x * r * r)


def next_row(x):
    return jnp.concatenate([x[1:], roll(x[:1], -1, 1)], 0)


def last_row(x):
    return jnp.concatenate([roll(x[-1:], 1, 1), x[:-1]], 0)


def kernel(
    sizes,
    tidx_hbm, tcur_hbm, dens_hbm, pad_hbm, row_hbm, col_hbm, mat_hbm, rates_hbm, theta_hbm, kappa_hbm, invc_hbm,
    drop_out, temp_out,
    tidx, tcur, mat, rates, ext, row_send, row_recv, col_send, xr, yr, coef, raw, ub, nat, unat,
    field, trow_send, trow, tcol_send, tx, ty, edge, heat_send, heat,
    temp_a, temp_b, east_a, east_b, west_a, west_b, aligned, cap, lx, ly, lw, lz, snat, stemp, scap, slx, sly, slz, sground, sheat, mix, begin, onat,
    isem, ssem, rsem, tssem, trsem, pssem, prsem,
):
    nx, ny, nz = sizes
    gx, gy, gz = lax.axis_index("gx"), lax.axis_index("gy"), lax.axis_index("gz")
    tiers, rows, cols = drop_out.shape
    layers = temp_out.shape[0]
    nc = ny * nz
    c = gy * nz + gz

    loads = [pltpu.make_async_copy(tidx_hbm, tidx, isem.at[0]), pltpu.make_async_copy(tcur_hbm, tcur, isem.at[1])]
    for a, ref in enumerate((dens_hbm, pad_hbm, row_hbm, col_hbm)):
        for tile in range(2):
            loads.append(pltpu.make_async_copy(
                ref.at[:, :, pl.ds(tile * 128, 128)], ext.at[a, :, tile, pl.ds(TOP, rows)], isem.at[len(loads)]
            ))
    loads.append(pltpu.make_async_copy(mat_hbm, mat, isem.at[len(loads)]))
    loads.append(pltpu.make_async_copy(rates_hbm, rates, isem.at[len(loads)]))
    heat_loads = [
        pltpu.make_async_copy(ref, field.at[a, :, pl.ds(8, rows)], isem.at[len(loads) + a])
        for a, ref in enumerate((theta_hbm, kappa_hbm, invc_hbm))
    ]

    def mesh_to(d):
        dx, dy = DIRS[d]
        return (lax.rem(gx + dx + nx, nx), lax.rem(gy + dy + ny, ny), gz)

    def heat_to(d):
        dx, dy = DIRS[d]
        there = lax.rem(c + dy + nc, nc)
        return (lax.rem(gx + dx + nx, nx), there // nz, lax.rem(there, nz))

    partner = (gx, gy, 1 - gz)

    barrier = pltpu.get_barrier_semaphore()
    for d in range(8):
        pl.semaphore_signal(barrier, inc=1, device_id=mesh_to(d), device_id_type=MESH)
    for d in range(2, 8):
        pl.semaphore_signal(barrier, inc=1, device_id=heat_to(d), device_id_type=MESH)
    for load in loads:
        load.start()

    def mesh_copy(d, p):
        t = pl.ds(2 * p, 2)
        top, bottom = pl.ds(0, TOP), pl.ds(rows - TOP, TOP)
        if d < 2:
            src, dst = row_send.at[d, t], row_recv.at[d, t]
        elif d == 2:
            src, dst = col_send.at[0, t], xr.at[t, pl.ds(TOP, rows)]
        elif d == 3:
            src, dst = col_send.at[1, t], yr.at[t, pl.ds(TOP, rows)]
        elif d == 4:
            src, dst = col_send.at[0, t, top], xr.at[t, pl.ds(TOP + rows, TOP)]
        elif d == 5:
            src, dst = col_send.at[1, t, top], yr.at[t, pl.ds(TOP + rows, TOP)]
        elif d == 6:
            src, dst = col_send.at[0, t, bottom], xr.at[t, pl.ds(0, TOP)]
        else:
            src, dst = col_send.at[1, t, bottom], yr.at[t, pl.ds(0, TOP)]
        return pltpu.make_async_remote_copy(
            src_ref=src, dst_ref=dst, send_sem=ssem.at[d, p], recv_sem=rsem.at[d, p],
            device_id=mesh_to(d), device_id_type=MESH,
        )

    def heat_copy(d):
        top, bottom = pl.ds(0, 8), pl.ds(rows - 8, 8)
        if d < 2:
            src, dst = trow_send.at[d], trow.at[d]
        elif d == 2:
            src, dst = tcol_send.at[0], tx.at[:, pl.ds(8, rows)]
        elif d == 3:
            src, dst = tcol_send.at[1], ty.at[:, pl.ds(8, rows)]
        elif d == 4:
            src, dst = tcol_send.at[0, :, top], tx.at[:, pl.ds(8 + rows, 8)]
        elif d == 5:
            src, dst = tcol_send.at[1, :, top], ty.at[:, pl.ds(8 + rows, 8)]
        elif d == 6:
            src, dst = tcol_send.at[0, :, bottom], tx.at[:, pl.ds(0, 8)]
        else:
            src, dst = tcol_send.at[1, :, bottom], ty.at[:, pl.ds(0, 8)]
        return pltpu.make_async_remote_copy(
            src_ref=src, dst_ref=dst, send_sem=tssem.at[d], recv_sem=trsem.at[d],
            device_id=heat_to(d), device_id_type=MESH,
        )

    def power_copy(t, z):
        return pltpu.make_async_remote_copy(
            src_ref=heat_send.at[t], dst_ref=heat.at[z * tiers + t], send_sem=pssem.at[t], recv_sem=prsem.at[t],
            device_id=partner, device_id_type=MESH,
        )

    def prepare(t):
        idx, cur = tidx[t], tcur[t]
        main = pl.ds(TOP, rows)
        lane = iota((rows, 128), 1)
        end_row = (iota((rows, 128), 0) == rows - 1) & (gx == nx - 1)
        end_col = (lane == 127) & (gy == ny - 1)
        edges = []
        for tile in range(2):
            spot = idx[tile : tile + 1]
            at_row = jnp.where(iota((rows, 128), 0) == (spot >> 7), cur[tile : tile + 1], 0.0)
            at_col = jnp.where(iota((128, 128), 0) == (spot & 127), 1.0, 0.0)
            taps = lax.dot_general(
                at_row, at_col, (((1,), (1,)), ((), ())),
                precision=lax.Precision.HIGHEST, preferred_element_type=F32,
            )
            source = ext[SRC, t, tile, main, :] + taps
            pad = ext[PAD, t, tile, main, :]
            gxp = jnp.where(end_row, 0.0, ext[GXP, t, tile, main, :])
            gyp = ext[GYP, t, tile, main, :]
            if tile == 1:
                gyp = jnp.where(end_col, 0.0, gyp)
            kinds = mat[t, :, tile * 128 : tile * 128 + 128]
            leak = jnp.zeros((rows, 128), F32)
            for kind in range(MATERIALS):
                leak = jnp.where(kinds == kind, rates[kind], leak)
            ext[SRC, t, tile, main, :] = source
            ext[GXP, t, tile, main, :] = gxp
            ext[GYP, t, tile, main, :] = gyp
            ext[LEAK, t, tile, main, :] = leak
            packed = jnp.zeros((rows, 128), F32)
            part = pl.ds(tile * 128, 128)
            for a, values in enumerate((source, pad, gxp, gyp, leak)):
                deep = DEEP if a < LEAK else 3
                at = a * DEEP
                row_send[0, t, at : at + deep, part] = values[:deep]
                row_send[1, t, at : at + deep, part] = values[rows - deep :]
                size = HALO if a < LEAK else 4
                mine = (lane >= a * PITCH) & (lane < a * PITCH + size)
                packed = jnp.where(mine, roll(values, a * PITCH + (size if tile else 0), 1), packed)
            row_send[0, t, 79:80, part] = jnp.zeros((1, 128), F32)
            row_send[1, t, 79:80, part] = jnp.zeros((1, 128), F32)
            col_send[tile, t] = packed

    def first_tiers(t, carry):
        prepare(t)

        @pl.when(t == 1)
        def _():
            pl.semaphore_wait(barrier, 14)

        @pl.when(t == 1)
        def _():
            for d in (4, 5, 6, 7, 0, 1, 2, 3):
                mesh_copy(d, 0).start()

        return carry

    for load in loads:
        load.wait()
    for load in heat_loads:
        load.start()
    lax.fori_loop(0, tiers, first_tiers, 0)

    lane_tall = iota((rows, 128), 1)
    sub = iota((16, 8, 128), 1)
    main = pl.ds(8, rows)
    for load in heat_loads:
        load.wait()
    for a in range(3):
        one, two = field[a, 0:16, 8:16, :], field[a, 16:32, 8:16, :]
        trow_send[0, a] = jnp.where(sub < 4, one, roll(two, 4, 1))
        one, two = field[a, 0:16, rows : rows + 8, :], field[a, 16:32, rows : rows + 8, :]
        trow_send[1, a] = jnp.where(sub < 4, roll(one, 4, 1), two)

    def gather(a, carry):
        low = high = jnp.zeros((rows, 128), F32)
        for l in range(16):
            mine = (lane_tall >> 3) == l
            low = jnp.where(mine, roll(field[a, l, main, :], 8 * l + 4, 1), low)
            high = jnp.where(mine, roll(field[a, l + 16, main, :], 8 * l + 4, 1), high)
        first = (lane_tall & 4) == 0
        tcol_send[0, a] = jnp.where(first, roll(high, -4, 1), low)
        tcol_send[1, a] = jnp.where(first, low, roll(high, 4, 1))
        edge[a, 0, main, :] = low
        edge[a, 1, main, :] = high
        return carry

    lax.fori_loop(0, 3, gather, 0)

    for d in range(8):
        mesh_copy(d, 0).wait_send()
    for d in (4, 5, 6, 7, 0, 1, 2, 3):
        mesh_copy(d, 1).start()
    for d in (4, 5, 6, 7, 2, 3, 0, 1):
        heat_copy(d).start()

    lane_ext = iota((8, 384), 1)
    inside = (lane_ext < cols + HALO) | (lane_ext >= 384 - HALO)
    lane_rows = iota((rows + 2 * TOP, 128), 1)
    lane_one = iota((8, 128), 1)
    half = lane_one < 64

    def halos(t, i):
        for a in range(5):
            size, deep = (HALO, DEEP) if a < LEAK else (4, 3)
            at = a * DEEP
            outside = jnp.full((TOP, 128), 1.0 if a == PAD else 0.0, F32)
            for tile in range(2):
                part = pl.ds(tile * 128, 128)
                ext[a, t, tile, 0:TOP, :] = outside
                ext[a, t, tile, TOP - deep : TOP, :] = row_recv[1, t, at : at + deep, part]
                ext[a, t, tile, TOP + rows :, :] = outside
                ext[a, t, tile, TOP + rows : TOP + rows + deep, :] = row_recv[0, t, at : at + deep, part]
            ext[a, t, 2] = jnp.where(
                lane_rows < 64, roll(xr[t], -a * PITCH, 1), roll(yr[t], 128 - size - a * PITCH, 1)
            )

        def fetch(a, start):
            return jnp.concatenate([ext[a, t, tile, pl.ds(start, 8, stride=V), :] for tile in range(3)], 1)

        gxm = fetch(GXP, TOP - HALO - 1)
        for v in range(V):
            src, pd, gxp, gyp, leak = [fetch(a, TOP - HALO + v) for a in range(5)]
            r = jnp.where(inside, inverse_root(pd + gxp + gxm + gyp + roll(gyp, 1, 1)), 0.0)
            gxm = gxp
            for j, x in enumerate((pd, gxp, gyp, leak, r)):
                raw[i, j, v] = x
            coef[i, 0, v] = src * r
            coef[i, 2, v] = gyp * r * roll(r, -1, 1)
        for v in range(V):
            after = raw[i, 4, v + 1] if v < V - 1 else roll(raw[i, 4, 0], -1, 0)
            coef[i, 1, v] = raw[i, 1, v] * raw[i, 4, v] * after
        coef[i, 1, V] = roll(coef[i, 1, V - 1], 1, 0)

    def sweep(source_of, i, out):
        here = source_of(0)
        before, link_before = roll(source_of(V - 1), 1, 0), coef[i, 1, V]
        for v in range(V):
            after = source_of(v + 1) if v < V - 1 else roll(source_of(0), -1, 0)
            link, side = coef[i, 1, v], coef[i, 2, v]
            flow = link * after + link_before * before
            flow = flow + (side * roll(here, -1, 1) + roll(side * here, 1, 1))
            ub[i, out, v] = coef[i, 0, v] + flow
            before, here, link_before = here, after, link

    def power_of(t, i):
        here = first = ub[i, 0, 0] * raw[i, 4, 0]
        for v in range(V):
            after = ub[i, 0, v + 1] * raw[i, 4, v + 1] if v < V - 1 else roll(first, -1, 0)
            across, along = after - here, roll(here, -1, 1) - here
            power = raw[i, 0, v] * here * here + raw[i, 1, v] * across * across + raw[i, 2, v] * along * along
            power = power + raw[i, 3, v] * jnp.exp(-here)
            at = pl.ds(TOP - HALO + v, 8, stride=V)
            for tile in range(3):
                nat[i, tile, at, :] = power[:, tile * 128 : tile * 128 + 128]
                if tile < 2:
                    unat[i, tile, at, :] = here[:, tile * 128 : tile * 128 + 128]
            here = after

        for z, into in ((1 - gz, heat_send.at[t]), (gz, heat.at[gz * tiers + t])):
            packed = jnp.zeros((8, 128), F32)
            for v in range(W):
                at = pl.ds(TOP - 4 + v, 8, stride=W)
                into[v] = nat[i, z, at, :]
                outer = jnp.where(half, nat[i, 1 + z, at, :], nat[i, 2 - 2 * z, at, :])
                packed = jnp.where((lane_one >> 3) == v, roll(outer, 8 * v + 4, 1), packed)
            into[W] = packed
        power_copy(t, gz).start()
        for tile in range(2):
            drop_out[t, :, tile * 128 : tile * 128 + 128] = unat[i, tile, TOP : TOP + rows, :]

    def pair(p, carry):
        def each(work):
            lax.fori_loop(0, 2, lambda i, held: (work(2 * p + i, i), held)[1], 0)

        for d in range(8):
            mesh_copy(d, p).wait_recv()
        each(halos)
        for i in range(2):
            sweep(lambda v: coef[i, 0, v], i, 0)

        def two_sweeps(count, held):
            for here in range(2):
                for i in range(2):
                    sweep(lambda v: ub[i, here, v], i, 1 - here)
            return held

        lax.fori_loop(0, (SWEEPS - 2) // 2, two_sweeps, 0)
        each(power_of)
        return carry

    lax.fori_loop(0, tiers // 2, pair, 0)

    for d in range(8):
        heat_copy(d).wait_recv()
    lane8 = iota((8, 128), 1)
    lane_tall = iota((rows + 16, 128), 1)
    first = (lane_tall & 4) == 0

    def assemble(a, carry):
        above, below = trow[1, a], trow[0, a]
        field[a, 0:16, 0:8, :] = roll(above, 4, 1)
        field[a, 16:32, 0:8, :] = above
        field[a, 0:16, 8 + rows : 16 + rows, :] = below
        field[a, 16:32, 8 + rows : 16 + rows, :] = roll(below, 4, 1)
        up = down = jnp.zeros((8, 128), F32)
        for l in range(16):
            mine = (lane8 >> 3) == l
            up = jnp.where(mine, roll(above[l], 8 * l + 4, 1), up)
            down = jnp.where(mine, roll(below[l], 8 * l + 4, 1), down)
        edge[a, 0, 0:8, :] = roll(up, 4, 0)
        edge[a, 1, 0:8, :] = up
        edge[a, 0, 8 + rows : 16 + rows, :] = down
        edge[a, 1, 8 + rows : 16 + rows, :] = roll(down, 4, 0)
        x, y, low, high = tx[a], ty[a], edge[a, 0], edge[a, 1]
        snat[a, 0] = jnp.where(first, y, low)
        snat[a, 1] = jnp.where(first, low, x)
        snat[a, 2] = jnp.where(first, roll(y, -4, 1), high)
        snat[a, 3] = jnp.where(first, high, roll(x, 4, 1))
        return carry

    lax.fori_loop(0, 3, assemble, 0)

    shape = (W, 8, 128)
    row_of = iota(shape, 1) * W + iota(shape, 0) - 4
    lane = iota(shape, 2)
    no_row = ((row_of == rows - 1) & (gx == nx - 1)) | ((row_of == -1) & (gx == 0))
    no_col = (lane == 127) & (c == nc - 1)

    def strided(ref):
        return jnp.stack([ref[pl.ds(4 + v, 8, stride=W), :] for v in range(W)])

    def upper(low, high):
        return jnp.where(lane < 120, roll(low, -8, 2), roll(high, -8, 2)), roll(high, -8, 2)

    def align(x, layer):
        return pltpu.roll(x, lax.rem(252 - 8 * lax.rem(layer, 16), 128), 2)

    for side in range(2):
        k = [strided(snat.at[1, 2 * h + side]) for h in range(2)]
        over = upper(*k)
        no_edge = ((lane & 7) == 3) & (c == (nc - 1 if side else 0))
        sground[side] = k[0]
        for h in range(2):
            s = 2 * h + side
            stemp[s] = strided(snat.at[0, s])
            scap[s] = strided(snat.at[2, s])
            slx[s] = jnp.where(no_row, 0.0, harmonic(k[h], next_row(k[h])))
            sly[s] = jnp.where(no_edge, 0.0, harmonic(k[h], roll(k[h], -1, 2)))
            link = harmonic(k[h], over[h])
            slz[s] = jnp.where(lane < 120, link, 0.0) if h else link
            if side:
                mix[h] = jnp.where((lane & 7) == 3, sly[2 * h], k[h])
                begin[h] = jnp.where((lane & 7) == 3, stemp[2 * h], stemp[s])

    def beside(x, beyond):
        right = roll(jnp.where(lane == 0, beyond, x), -1, 2)
        left = roll(jnp.where(lane == 127, beyond, x), 1, 2)
        return right, left

    def bring(layer, carry):
        aligned[layer] = align(begin[layer // 16], layer)
        east_b[layer] = align(mix[layer // 16], layer)
        return carry

    lax.fori_loop(0, layers, bring, 0, unroll=4)

    def links(layer, k):
        x = strided(field.at[0, layer])
        temp_a[layer] = x
        east_a[layer], west_a[layer] = beside(x, aligned[layer])
        cap[layer] = strided(field.at[2, layer])
        over = strided(field.at[1, jnp.minimum(layer + 1, layers - 1)])
        beyond = east_b[layer]
        right = harmonic(k, roll(jnp.where(lane == 0, beyond, k), -1, 2))
        right = jnp.where(no_col, 0.0, right)
        lx[layer] = jnp.where(no_row, 0.0, harmonic(k, next_row(k)))
        ly[layer] = right
        lw[layer] = roll(jnp.where(lane == 127, beyond, right), 1, 2)
        lz[layer + 1] = jnp.where(layer == layers - 1, 0.0, harmonic(k, over))
        return over

    ground = strided(field.at[1, 0])
    lz[0] = ground
    lax.fori_loop(0, layers, links, ground, unroll=4)

    for t in range(tiers):
        power_copy(t, 1 - gz).wait()

    for h in range(2):
        left = right = jnp.zeros(shape, F32)
        for t in range(4):
            inner, packed = heat[h * 4 + t, 0:W], heat[h * 4 + t, W]
            outer = jnp.stack([roll(packed, -8 * v - 4, 1) for v in range(W)])
            mine = (lane >> 3) == 4 * t
            left = jnp.where(mine, roll(jnp.where(lane < 64, inner, outer), 32 * t + 4, 2), left)
            right = jnp.where(mine, roll(jnp.where(lane < 64, outer, inner), 32 * t + 4, 2), right)
        sheat[2 * h] = left
        sheat[2 * h + 1] = right

    def strips():
        for side in range(2):
            old = [stemp[side], stemp[2 + side]]
            over = upper(*old)
            rise = [slz[2 * h + side] * (over[h] - old[h]) for h in range(2)]
            under = (
                jnp.where(lane < 8, sground[side] * old[0], roll(rise[0], 8, 2)),
                jnp.where(lane < 8, roll(rise[0], 8, 2), roll(rise[1], 8, 2)),
            )
            for h in range(2):
                s = 2 * h + side
                here = old[h]
                fx = slx[s] * (next_row(here) - here)
                fy = sly[s] * (roll(here, -1, 2) - here)
                flow = (fx - last_row(fx)) + (fy - roll(fy, 1, 2)) + (rise[h] - under[h]) + sheat[s]
                after = here + scap[s] * flow
                stemp[s] = after
                mix[h] = jnp.where((lane & 7) == 3, mix[h], after) if side else after

    def shift(layer, state):
        temp, east, west = state
        east[layer], west[layer] = beside(temp[layer], aligned[layer])

    states = ((temp_a, east_a, west_a), (temp_b, east_b, west_b))
    for count in range(STEPS):
        now, then, more = states[count % 2], states[1 - count % 2], count < STEPS - 1
        if more:
            strips()
        if count:
            for layer in range(layers - 4, layers):
                shift(layer, now)

        def group(g, below, now=now, then=then, more=more):
            temp, east, west = now
            base = 4 * g
            if more:
                for part in range(4):
                    shift(4 * jnp.maximum(g - 1, 0) + part, then)
            for part in range(4):
                layer = base + part
                over = layer + 1 if part < 3 else jnp.minimum(layer + 1, layers - 1)
                fx_last = roll(lx[layer, W - 1] * (roll(temp[layer, 0], -1, 0) - temp[layer, W - 1]), 1, 0)
                rise = []
                for v in range(W):
                    here = temp[layer, v]
                    after = temp[layer, v + 1] if v < W - 1 else roll(temp[layer, 0], -1, 0)
                    fx = lx[layer, v] * (after - here)
                    fz = lz[layer + 1, v] * (temp[over, v] - here)
                    flow = ly[layer, v] * (east[layer, v] - here) + lw[layer, v] * (west[layer, v] - here)
                    flow = flow + (fx - fx_last) + (fz - below[v])
                    if part == 0:
                        flow = flow + heat[g, v]
                    then[0][layer, v] = here + cap[layer, v] * flow
                    fx_last = fx
                    rise.append(fz)
                below = tuple(rise)
                if more:
                    aligned[layer] = align(mix[g // 4], layer)
            return below

        lax.fori_loop(0, layers // 4, group, tuple(lz[0, v] * now[0][0, v] for v in range(W)))

    def result(layer, carry):
        for v in range(W):
            onat[layer, pl.ds(4 + v, 8, stride=W), :] = states[STEPS % 2][0][layer, v]
        temp_out[layer] = onat[layer, pl.ds(8, rows), :]
        return carry

    lax.fori_loop(0, layers, result, 0, unroll=4)

    for d in range(8):
        heat_copy(d).wait_send()
    for d in range(8):
        mesh_copy(d, 1).wait_send()


def shards(sizes, density, tap_index, tap_current, pad_cond, row_cond, col_cond, material, leak_rates, theta, kappa, invc):
    tiers, rows, cols = density.shape
    layers = theta.shape[0]
    vmem, hbm = pl.BlockSpec(memory_space=pltpu.VMEM), pl.BlockSpec(memory_space=pltpu.HBM)
    tall, high = rows + 2 * TOP, rows + 16
    dma = pltpu.SemaphoreType.DMA
    taps = tap_index.shape[-1]
    scratch = [
        (5, tiers, 3, tall, 128),
        (2, tiers, 80, cols), (2, tiers, 80, cols), (2, tiers, rows, 128),
        (tiers, tall, 128), (tiers, tall, 128),
        (2, 3, V + 1, 8, 384), (2, 5, V, 8, 384), (2, 2, V, 8, 384),
        (2, 3, tall, 128), (2, 2, tall, 128),
        (3, layers, high, 128),
        (2, 3, 16, 8, 128), (2, 3, 16, 8, 128),
        (2, 3, rows, 128), (3, high, 128), (3, high, 128), (3, 2, high, 128),
        (tiers, W + 1, 8, 128), (2 * tiers, W + 1, 8, 128),
        *[(layers, W, 8, 128)] * 6,
        (layers, W, 8, 128), (layers, W, 8, 128),
        (layers, W, 8, 128), (layers, W, 8, 128), (layers, W, 8, 128), (layers + 1, W, 8, 128),
        (3, 4, high, 128),
        (4, W, 8, 128), (4, W, 8, 128), (4, W, 8, 128), (4, W, 8, 128), (4, W, 8, 128),
        (2, W, 8, 128), (4, W, 8, 128), (2, W, 8, 128), (2, W, 8, 128),
        (layers, high, 128),
    ]
    return pl.pallas_call(
        functools.partial(kernel, sizes),
        out_shape=(jax.ShapeDtypeStruct((tiers, rows, cols), F32), jax.ShapeDtypeStruct(theta.shape, F32)),
        in_specs=[hbm] * 11,
        out_specs=(vmem, vmem),
        scratch_shapes=[
            pltpu.VMEM((tiers, 2, taps), jnp.int32),
            pltpu.VMEM((tiers, 2, taps), F32),
            pltpu.VMEM((tiers, rows, cols), jnp.int32),
            pltpu.SMEM((MATERIALS,), F32),
            *[pltpu.VMEM(size, F32) for size in scratch],
            dma((15,)), dma((8, tiers // 2)), dma((8, tiers // 2)), dma((8,)), dma((8,)), dma((tiers,)), dma((tiers,)),
        ],
        compiler_params=pltpu.CompilerParams(
            collective_id=0, has_side_effects=True, vmem_limit_bytes=34 * 2**20
        ),
        name="electrothermal",
    )(
        *[pltpu.with_memory_space_constraint(x, pltpu.HBM) for x in (
            tap_index.reshape(tiers, 2, taps), tap_current.reshape(tiers, 2, taps), density, pad_cond, row_cond,
            col_cond, material, leak_rates, theta, kappa, invc,
        )],
    )


def solution(mesh):
    sizes = tuple(mesh.shape[name] for name in ("gx", "gy", "gz"))
    mesh_field = P("gz", "gx", "gy")
    tap = P("gz", "gx", "gy", None)
    block = P(None, "gx", ("gy", "gz"))
    return jax.shard_map(
        functools.partial(shards, sizes),
        mesh=mesh,
        in_specs=(mesh_field, tap, tap, mesh_field, mesh_field, mesh_field, mesh_field, P(), block, block, block),
        out_specs=(mesh_field, block),
        check_vma=False,
    )
```

```python
import functools

import jax
import jax.numpy as jnp
from jax import lax
from jax.experimental import pallas as pl
from jax.experimental.pallas import tpu as pltpu
from jax.sharding import PartitionSpec as P

MESH = pl.DeviceIdType.MESH
F32 = jnp.float32
SWEEPS = 16
STEPS = 4
MATERIALS = 4
HALO = 20
DEEP = 19
PITCH = 24
TOP = 24
V = 13
W = 9
SRC, PAD, GXP, GYP, LEAK = range(5)
DIRS = ((-1, 0), (1, 0), (0, -1), (0, 1), (-1, -1), (-1, 1), (1, -1), (1, 1))


def iota(shape, dim):
    return lax.broadcasted_iota(jnp.int32, shape, dim)


def roll(x, shift, axis):
    return pltpu.roll(x, shift % x.shape[axis], axis)


def harmonic(a, b):
    total = a + b
    r = pl.reciprocal(total, approx=True)
    r = r * (2.0 - total * r)
    r = r * (2.0 - total * r)
    return 2.0 * a * b * r


def inverse_root(x):
    r = lax.rsqrt(x)
    return r * (1.5 - 0.5 * x * r * r)


def next_row(x):
    return jnp.concatenate([x[1:], roll(x[:1], -1, 1)], 0)


def last_row(x):
    return jnp.concatenate([roll(x[-1:], 1, 1), x[:-1]], 0)


def kernel(
    sizes,
    tidx_hbm, tcur_hbm, dens_hbm, pad_hbm, row_hbm, col_hbm, mat_hbm, rates_hbm, theta_hbm, kappa_hbm, invc_hbm,
    drop_out, temp_out,
    tidx, tcur, mat, rates, ext, row_send, row_recv, col_send, xr, yr, coef, raw, ub, nat, unat,
    field, trow_send, trow, tcol_send, tx, ty, edge, heat_send, heat,
    temp_a, temp_b, east_a, east_b, west_a, west_b, aligned, cap, lx, ly, lw, lz, snat, stemp, scap, slx, sly, slz, sground, sheat, mix, begin, onat,
    isem, ssem, rsem, tssem, trsem, pssem, prsem,
):
    nx, ny, nz = sizes
    gx, gy, gz = lax.axis_index("gx"), lax.axis_index("gy"), lax.axis_index("gz")
    tiers, rows, cols = drop_out.shape
    layers = temp_out.shape[0]
    nc = ny * nz
    c = gy * nz + gz

    loads = [pltpu.make_async_copy(tidx_hbm, tidx, isem.at[0]), pltpu.make_async_copy(tcur_hbm, tcur, isem.at[1])]
    for a, ref in enumerate((dens_hbm, pad_hbm, row_hbm, col_hbm)):
        for tile in range(2):
            loads.append(pltpu.make_async_copy(
                ref.at[:, :, pl.ds(tile * 128, 128)], ext.at[a, :, tile, pl.ds(TOP, rows)], isem.at[len(loads)]
            ))
    loads.append(pltpu.make_async_copy(mat_hbm, mat, isem.at[len(loads)]))
    loads.append(pltpu.make_async_copy(rates_hbm, rates, isem.at[len(loads)]))
    heat_loads = [
        pltpu.make_async_copy(ref, field.at[a, :, pl.ds(8, rows)], isem.at[len(loads) + a])
        for a, ref in enumerate((theta_hbm, kappa_hbm, invc_hbm))
    ]

    def mesh_to(d):
        dx, dy = DIRS[d]
        return (lax.rem(gx + dx + nx, nx), lax.rem(gy + dy + ny, ny), gz)

    def heat_to(d):
        dx, dy = DIRS[d]
        there = lax.rem(c + dy + nc, nc)
        return (lax.rem(gx + dx + nx, nx), there // nz, lax.rem(there, nz))

    partner = (gx, gy, 1 - gz)

    barrier = pltpu.get_barrier_semaphore()
    for d in range(8):
        pl.semaphore_signal(barrier, inc=1, device_id=mesh_to(d), device_id_type=MESH)
    for d in range(2, 8):
        pl.semaphore_signal(barrier, inc=1, device_id=heat_to(d), device_id_type=MESH)
    for load in loads:
        load.start()

    def mesh_copy(d, p):
        t = pl.ds(2 * p, 2)
        top, bottom = pl.ds(0, TOP), pl.ds(rows - TOP, TOP)
        if d < 2:
            src, dst = row_send.at[d, t], row_recv.at[d, t]
        elif d == 2:
            src, dst = col_send.at[0, t], xr.at[t, pl.ds(TOP, rows)]
        elif d == 3:
            src, dst = col_send.at[1, t], yr.at[t, pl.ds(TOP, rows)]
        elif d == 4:
            src, dst = col_send.at[0, t, top], xr.at[t, pl.ds(TOP + rows, TOP)]
        elif d == 5:
            src, dst = col_send.at[1, t, top], yr.at[t, pl.ds(TOP + rows, TOP)]
        elif d == 6:
            src, dst = col_send.at[0, t, bottom], xr.at[t, pl.ds(0, TOP)]
        else:
            src, dst = col_send.at[1, t, bottom], yr.at[t, pl.ds(0, TOP)]
        return pltpu.make_async_remote_copy(
            src_ref=src, dst_ref=dst, send_sem=ssem.at[d, p], recv_sem=rsem.at[d, p],
            device_id=mesh_to(d), device_id_type=MESH,
        )

    def heat_copy(d):
        top, bottom = pl.ds(0, 8), pl.ds(rows - 8, 8)
        if d < 2:
            src, dst = trow_send.at[d], trow.at[d]
        elif d == 2:
            src, dst = tcol_send.at[0], tx.at[:, pl.ds(8, rows)]
        elif d == 3:
            src, dst = tcol_send.at[1], ty.at[:, pl.ds(8, rows)]
        elif d == 4:
            src, dst = tcol_send.at[0, :, top], tx.at[:, pl.ds(8 + rows, 8)]
        elif d == 5:
            src, dst = tcol_send.at[1, :, top], ty.at[:, pl.ds(8 + rows, 8)]
        elif d == 6:
            src, dst = tcol_send.at[0, :, bottom], tx.at[:, pl.ds(0, 8)]
        else:
            src, dst = tcol_send.at[1, :, bottom], ty.at[:, pl.ds(0, 8)]
        return pltpu.make_async_remote_copy(
            src_ref=src, dst_ref=dst, send_sem=tssem.at[d], recv_sem=trsem.at[d],
            device_id=heat_to(d), device_id_type=MESH,
        )

    def power_copy(t, z):
        return pltpu.make_async_remote_copy(
            src_ref=heat_send.at[t], dst_ref=heat.at[z * tiers + t], send_sem=pssem.at[t], recv_sem=prsem.at[t],
            device_id=partner, device_id_type=MESH,
        )

    def prepare(t):
        idx, cur = tidx[t], tcur[t]
        main = pl.ds(TOP, rows)
        lane = iota((rows, 128), 1)
        end_row = (iota((rows, 128), 0) == rows - 1) & (gx == nx - 1)
        end_col = (lane == 127) & (gy == ny - 1)
        edges = []
        for tile in range(2):
            spot = idx[tile : tile + 1]
            at_row = jnp.where(iota((rows, 128), 0) == (spot >> 7), cur[tile : tile + 1], 0.0)
            at_col = jnp.where(iota((128, 128), 0) == (spot & 127), 1.0, 0.0)
            taps = lax.dot_general(
                at_row, at_col, (((1,), (1,)), ((), ())),
                precision=lax.Precision.HIGHEST, preferred_element_type=F32,
            )
            source = ext[SRC, t, tile, main, :] + taps
            pad = ext[PAD, t, tile, main, :]
            gxp = jnp.where(end_row, 0.0, ext[GXP, t, tile, main, :])
            gyp = ext[GYP, t, tile, main, :]
            if tile == 1:
                gyp = jnp.where(end_col, 0.0, gyp)
            kinds = mat[t, :, tile * 128 : tile * 128 + 128]
            leak = jnp.zeros((rows, 128), F32)
            for kind in range(MATERIALS):
                leak = jnp.where(kinds == kind, rates[kind], leak)
            ext[SRC, t, tile, main, :] = source
            ext[GXP, t, tile, main, :] = gxp
            ext[GYP, t, tile, main, :] = gyp
            ext[LEAK, t, tile, main, :] = leak
            packed = jnp.zeros((rows, 128), F32)
            part = pl.ds(tile * 128, 128)
            for a, values in enumerate((source, pad, gxp, gyp, leak)):
                deep = DEEP if a < LEAK else 3
                at = a * DEEP
                row_send[0, t, at : at + deep, part] = values[:deep]
                row_send[1, t, at : at + deep, part] = values[rows - deep :]
                size = HALO if a < LEAK else 4
                mine = (lane >= a * PITCH) & (lane < a * PITCH + size)
                packed = jnp.where(mine, roll(values, a * PITCH + (size if tile else 0), 1), packed)
            row_send[0, t, 79:80, part] = jnp.zeros((1, 128), F32)
            row_send[1, t, 79:80, part] = jnp.zeros((1, 128), F32)
            col_send[tile, t] = packed

    def first_tiers(t, carry):
        prepare(t)

        @pl.when(t == 1)
        def _():
            pl.semaphore_wait(barrier, 14)

        @pl.when(t == 1)
        def _():
            for d in (4, 5, 6, 7, 0, 1, 2, 3):
                mesh_copy(d, 0).start()

        return carry

    for load in loads:
        load.wait()
    for load in heat_loads:
        load.start()
    lax.fori_loop(0, tiers, first_tiers, 0)

    lane_tall = iota((rows, 128), 1)
    sub = iota((16, 8, 128), 1)
    main = pl.ds(8, rows)
    for load in heat_loads:
        load.wait()
    for a in range(3):
        one, two = field[a, 0:16, 8:16, :], field[a, 16:32, 8:16, :]
        trow_send[0, a] = jnp.where(sub < 4, one, roll(two, 4, 1))
        one, two = field[a, 0:16, rows : rows + 8, :], field[a, 16:32, rows : rows + 8, :]
        trow_send[1, a] = jnp.where(sub < 4, roll(one, 4, 1), two)

    def gather(a, carry):
        low = high = jnp.zeros((rows, 128), F32)
        for l in range(16):
            mine = (lane_tall >> 3) == l
            low = jnp.where(mine, roll(field[a, l, main, :], 8 * l + 4, 1), low)
            high = jnp.where(mine, roll(field[a, l + 16, main, :], 8 * l + 4, 1), high)
        first = (lane_tall & 4) == 0
        tcol_send[0, a] = jnp.where(first, roll(high, -4, 1), low)
        tcol_send[1, a] = jnp.where(first, low, roll(high, 4, 1))
        edge[a, 0, main, :] = low
        edge[a, 1, main, :] = high
        return carry

    lax.fori_loop(0, 3, gather, 0)

    for d in range(8):
        mesh_copy(d, 0).wait_send()
    for d in (4, 5, 6, 7, 0, 1, 2, 3):
        mesh_copy(d, 1).start()
    for d in (4, 5, 6, 7, 2, 3, 0, 1):
        heat_copy(d).start()

    lane_ext = iota((8, 384), 1)
    inside = (lane_ext < cols + HALO) | (lane_ext >= 384 - HALO)
    lane_rows = iota((rows + 2 * TOP, 128), 1)
    lane_one = iota((8, 128), 1)
    half = lane_one < 64

    def halos(t, i):
        for a in range(5):
            size, deep = (HALO, DEEP) if a < LEAK else (4, 3)
            at = a * DEEP
            outside = jnp.full((TOP, 128), 1.0 if a == PAD else 0.0, F32)
            for tile in range(2):
                part = pl.ds(tile * 128, 128)
                ext[a, t, tile, 0:TOP, :] = outside
                ext[a, t, tile, TOP - deep : TOP, :] = row_recv[1, t, at : at + deep, part]
                ext[a, t, tile, TOP + rows :, :] = outside
                ext[a, t, tile, TOP + rows : TOP + rows + deep, :] = row_recv[0, t, at : at + deep, part]
            ext[a, t, 2] = jnp.where(
                lane_rows < 64, roll(xr[t], -a * PITCH, 1), roll(yr[t], 128 - size - a * PITCH, 1)
            )

        def fetch(a, start):
            return jnp.concatenate([ext[a, t, tile, pl.ds(start, 8, stride=V), :] for tile in range(3)], 1)

        gxm = fetch(GXP, TOP - HALO - 1)
        for v in range(V):
            src, pd, gxp, gyp, leak = [fetch(a, TOP - HALO + v) for a in range(5)]
            r = jnp.where(inside, inverse_root(pd + gxp + gxm + gyp + roll(gyp, 1, 1)), 0.0)
            gxm = gxp
            for j, x in enumerate((pd, gxp, gyp, leak, r)):
                raw[i, j, v] = x
            coef[i, 0, v] = src * r
            coef[i, 2, v] = gyp * r * roll(r, -1, 1)
        for v in range(V):
            after = raw[i, 4, v + 1] if v < V - 1 else roll(raw[i, 4, 0], -1, 0)
            coef[i, 1, v] = raw[i, 1, v] * raw[i, 4, v] * after
        coef[i, 1, V] = roll(coef[i, 1, V - 1], 1, 0)

    def sweep(source_of, i, out):
        here = source_of(0)
        before, link_before = roll(source_of(V - 1), 1, 0), coef[i, 1, V]
        for v in range(V):
            after = source_of(v + 1) if v < V - 1 else roll(source_of(0), -1, 0)
            link, side = coef[i, 1, v], coef[i, 2, v]
            flow = link * after + link_before * before
            flow = flow + (side * roll(here, -1, 1) + roll(side * here, 1, 1))
            ub[i, out, v] = coef[i, 0, v] + flow
            before, here, link_before = here, after, link

    def power_of(t, i):
        here = first = ub[i, 0, 0] * raw[i, 4, 0]
        for v in range(V):
            after = ub[i, 0, v + 1] * raw[i, 4, v + 1] if v < V - 1 else roll(first, -1, 0)
            across, along = after - here, roll(here, -1, 1) - here
            power = raw[i, 0, v] * here * here + raw[i, 1, v] * across * across + raw[i, 2, v] * along * along
            power = power + raw[i, 3, v] * jnp.exp(-here)
            at = pl.ds(TOP - HALO + v, 8, stride=V)
            for tile in range(3):
                nat[i, tile, at, :] = power[:, tile * 128 : tile * 128 + 128]
                if tile < 2:
                    unat[i, tile, at, :] = here[:, tile * 128 : tile * 128 + 128]
            here = after

        for z, into in ((1 - gz, heat_send.at[t]), (gz, heat.at[gz * tiers + t])):
            packed = jnp.zeros((8, 128), F32)
            for v in range(W):
                at = pl.ds(TOP - 4 + v, 8, stride=W)
                into[v] = nat[i, z, at, :]
                outer = jnp.where(half, nat[i, 1 + z, at, :], nat[i, 2 - 2 * z, at, :])
                packed = jnp.where((lane_one >> 3) == v, roll(outer, 8 * v + 4, 1), packed)
            into[W] = packed
        power_copy(t, gz).start()
        for tile in range(2):
            drop_out[t, :, tile * 128 : tile * 128 + 128] = unat[i, tile, TOP : TOP + rows, :]

    def pair(p, carry):
        def each(work):
            lax.fori_loop(0, 2, lambda i, held: (work(2 * p + i, i), held)[1], 0)

        for d in range(8):
            mesh_copy(d, p).wait_recv()
        each(halos)
        for i in range(2):
            sweep(lambda v: coef[i, 0, v], i, 0)

        def two_sweeps(count, held):
            for here in range(2):
                for i in range(2):
                    sweep(lambda v: ub[i, here, v], i, 1 - here)
            return held

        lax.fori_loop(0, (SWEEPS - 2) // 2, two_sweeps, 0)
        each(power_of)
        return carry

    lax.fori_loop(0, tiers // 2, pair, 0)

    for d in range(8):
        heat_copy(d).wait_recv()
    lane8 = iota((8, 128), 1)
    lane_tall = iota((rows + 16, 128), 1)
    first = (lane_tall & 4) == 0

    def assemble(a, carry):
        above, below = trow[1, a], trow[0, a]
        field[a, 0:16, 0:8, :] = roll(above, 4, 1)
        field[a, 16:32, 0:8, :] = above
        field[a, 0:16, 8 + rows : 16 + rows, :] = below
        field[a, 16:32, 8 + rows : 16 + rows, :] = roll(below, 4, 1)
        up = down = jnp.zeros((8, 128), F32)
        for l in range(16):
            mine = (lane8 >> 3) == l
            up = jnp.where(mine, roll(above[l], 8 * l + 4, 1), up)
            down = jnp.where(mine, roll(below[l], 8 * l + 4, 1), down)
        edge[a, 0, 0:8, :] = roll(up, 4, 0)
        edge[a, 1, 0:8, :] = up
        edge[a, 0, 8 + rows : 16 + rows, :] = down
        edge[a, 1, 8 + rows : 16 + rows, :] = roll(down, 4, 0)
        x, y, low, high = tx[a], ty[a], edge[a, 0], edge[a, 1]
        snat[a, 0] = jnp.where(first, y, low)
        snat[a, 1] = jnp.where(first, low, x)
        snat[a, 2] = jnp.where(first, roll(y, -4, 1), high)
        snat[a, 3] = jnp.where(first, high, roll(x, 4, 1))
        return carry

    lax.fori_loop(0, 3, assemble, 0)

    shape = (W, 8, 128)
    row_of = iota(shape, 1) * W + iota(shape, 0) - 4
    lane = iota(shape, 2)
    no_row = ((row_of == rows - 1) & (gx == nx - 1)) | ((row_of == -1) & (gx == 0))
    no_col = (lane == 127) & (c == nc - 1)

    def strided(ref):
        return jnp.stack([ref[pl.ds(4 + v, 8, stride=W), :] for v in range(W)])

    def upper(low, high):
        return jnp.where(lane < 120, roll(low, -8, 2), roll(high, -8, 2)), roll(high, -8, 2)

    def align(x, layer):
        return pltpu.roll(x, lax.rem(252 - 8 * lax.rem(layer, 16), 128), 2)

    for side in range(2):
        k = [strided(snat.at[1, 2 * h + side]) for h in range(2)]
        over = upper(*k)
        no_edge = ((lane & 7) == 3) & (c == (nc - 1 if side else 0))
        sground[side] = k[0]
        for h in range(2):
            s = 2 * h + side
            stemp[s] = strided(snat.at[0, s])
            scap[s] = strided(snat.at[2, s])
            slx[s] = jnp.where(no_row, 0.0, harmonic(k[h], next_row(k[h])))
            sly[s] = jnp.where(no_edge, 0.0, harmonic(k[h], roll(k[h], -1, 2)))
            link = harmonic(k[h], over[h])
            slz[s] = jnp.where(lane < 120, link, 0.0) if h else link
            if side:
                mix[h] = jnp.where((lane & 7) == 3, sly[2 * h], k[h])
                begin[h] = jnp.where((lane & 7) == 3, stemp[2 * h], stemp[s])

    def beside(x, beyond):
        right = roll(jnp.where(lane == 0, beyond, x), -1, 2)
        left = roll(jnp.where(lane == 127, beyond, x), 1, 2)
        return right, left

    def bring(layer, carry):
        aligned[layer] = align(begin[layer // 16], layer)
        east_b[layer] = align(mix[layer // 16], layer)
        return carry

    lax.fori_loop(0, layers, bring, 0, unroll=4)

    def links(layer, k):
        x = strided(field.at[0, layer])
        temp_a[layer] = x
        east_a[layer], west_a[layer] = beside(x, aligned[layer])
        cap[layer] = strided(field.at[2, layer])
        over = strided(field.at[1, jnp.minimum(layer + 1, layers - 1)])
        beyond = east_b[layer]
        right = harmonic(k, roll(jnp.where(lane == 0, beyond, k), -1, 2))
        right = jnp.where(no_col, 0.0, right)
        lx[layer] = jnp.where(no_row, 0.0, harmonic(k, next_row(k)))
        ly[layer] = right
        lw[layer] = roll(jnp.where(lane == 127, beyond, right), 1, 2)
        lz[layer + 1] = jnp.where(layer == layers - 1, 0.0, harmonic(k, over))
        return over

    ground = strided(field.at[1, 0])
    lz[0] = ground
    lax.fori_loop(0, layers, links, ground, unroll=4)

    for t in range(tiers):
        power_copy(t, 1 - gz).wait()

    for h in range(2):
        left = right = jnp.zeros(shape, F32)
        for t in range(4):
            inner, packed = heat[h * 4 + t, 0:W], heat[h * 4 + t, W]
            outer = jnp.stack([roll(packed, -8 * v - 4, 1) for v in range(W)])
            mine = (lane >> 3) == 4 * t
            left = jnp.where(mine, roll(jnp.where(lane < 64, inner, outer), 32 * t + 4, 2), left)
            right = jnp.where(mine, roll(jnp.where(lane < 64, outer, inner), 32 * t + 4, 2), right)
        sheat[2 * h] = left
        sheat[2 * h + 1] = right

    def strips():
        for side in range(2):
            old = [stemp[side], stemp[2 + side]]
            over = upper(*old)
            rise = [slz[2 * h + side] * (over[h] - old[h]) for h in range(2)]
            under = (
                jnp.where(lane < 8, sground[side] * old[0], roll(rise[0], 8, 2)),
                jnp.where(lane < 8, roll(rise[0], 8, 2), roll(rise[1], 8, 2)),
            )
            for h in range(2):
                s = 2 * h + side
                here = old[h]
                fx = slx[s] * (next_row(here) - here)
                fy = sly[s] * (roll(here, -1, 2) - here)
                flow = (fx - last_row(fx)) + (fy - roll(fy, 1, 2)) + (rise[h] - under[h]) + sheat[s]
                after = here + scap[s] * flow
                stemp[s] = after
                mix[h] = jnp.where((lane & 7) == 3, mix[h], after) if side else after

    def shift(layer, state):
        temp, east, west = state
        east[layer], west[layer] = beside(temp[layer], aligned[layer])

    states = ((temp_a, east_a, west_a), (temp_b, east_b, west_b))
    for count in range(STEPS):
        now, then, more = states[count % 2], states[1 - count % 2], count < STEPS - 1
        if more:
            strips()
        if count:
            for layer in range(layers - 4, layers):
                shift(layer, now)

        def group(g, below, now=now, then=then, more=more):
            temp, east, west = now
            base = 4 * g
            if more:
                for part in range(4):
                    shift(4 * jnp.maximum(g - 1, 0) + part, then)
            for part in range(4):
                layer = base + part
                over = layer + 1 if part < 3 else jnp.minimum(layer + 1, layers - 1)
                fx_last = roll(lx[layer, W - 1] * (roll(temp[layer, 0], -1, 0) - temp[layer, W - 1]), 1, 0)
                rise = []
                for v in range(W):
                    here = temp[layer, v]
                    after = temp[layer, v + 1] if v < W - 1 else roll(temp[layer, 0], -1, 0)
                    fx = lx[layer, v] * (after - here)
                    fz = lz[layer + 1, v] * (temp[over, v] - here)
                    flow = ly[layer, v] * (east[layer, v] - here) + lw[layer, v] * (west[layer, v] - here)
                    flow = flow + (fx - fx_last) + (fz - below[v])
                    if part == 0:
                        flow = flow + heat[g, v]
                    if more:
                        then[0][layer, v] = here + cap[layer, v] * flow
                    else:
                        onat[layer, pl.ds(4 + v, 8, stride=W), :] = here + cap[layer, v] * flow
                    fx_last = fx
                    rise.append(fz)
                below = tuple(rise)
                if more:
                    aligned[layer] = align(mix[g // 4], layer)
            return below

        lax.fori_loop(0, layers // 4, group, tuple(lz[0, v] * now[0][0, v] for v in range(W)))

    def result(layer, carry):
        temp_out[layer] = onat[layer, pl.ds(8, rows), :]
        return carry

    lax.fori_loop(0, layers, result, 0, unroll=4)

    for d in range(8):
        heat_copy(d).wait_send()
    for d in range(8):
        mesh_copy(d, 1).wait_send()


def shards(sizes, density, tap_index, tap_current, pad_cond, row_cond, col_cond, material, leak_rates, theta, kappa, invc):
    tiers, rows, cols = density.shape
    layers = theta.shape[0]
    vmem, hbm = pl.BlockSpec(memory_space=pltpu.VMEM), pl.BlockSpec(memory_space=pltpu.HBM)
    tall, high = rows + 2 * TOP, rows + 16
    dma = pltpu.SemaphoreType.DMA
    taps = tap_index.shape[-1]
    scratch = [
        (5, tiers, 3, tall, 128),
        (2, tiers, 80, cols), (2, tiers, 80, cols), (2, tiers, rows, 128),
        (tiers, tall, 128), (tiers, tall, 128),
        (2, 3, V + 1, 8, 384), (2, 5, V, 8, 384), (2, 2, V, 8, 384),
        (2, 3, tall, 128), (2, 2, tall, 128),
        (3, layers, high, 128),
        (2, 3, 16, 8, 128), (2, 3, 16, 8, 128),
        (2, 3, rows, 128), (3, high, 128), (3, high, 128), (3, 2, high, 128),
        (tiers, W + 1, 8, 128), (2 * tiers, W + 1, 8, 128),
        *[(layers, W, 8, 128)] * 6,
        (layers, W, 8, 128), (layers, W, 8, 128),
        (layers, W, 8, 128), (layers, W, 8, 128), (layers, W, 8, 128), (layers + 1, W, 8, 128),
        (3, 4, high, 128),
        (4, W, 8, 128), (4, W, 8, 128), (4, W, 8, 128), (4, W, 8, 128), (4, W, 8, 128),
        (2, W, 8, 128), (4, W, 8, 128), (2, W, 8, 128), (2, W, 8, 128),
        (layers, high, 128),
    ]
    return pl.pallas_call(
        functools.partial(kernel, sizes),
        out_shape=(jax.ShapeDtypeStruct((tiers, rows, cols), F32), jax.ShapeDtypeStruct(theta.shape, F32)),
        in_specs=[hbm] * 11,
        out_specs=(vmem, vmem),
        scratch_shapes=[
            pltpu.VMEM((tiers, 2, taps), jnp.int32),
            pltpu.VMEM((tiers, 2, taps), F32),
            pltpu.VMEM((tiers, rows, cols), jnp.int32),
            pltpu.SMEM((MATERIALS,), F32),
            *[pltpu.VMEM(size, F32) for size in scratch],
            dma((15,)), dma((8, tiers // 2)), dma((8, tiers // 2)), dma((8,)), dma((8,)), dma((tiers,)), dma((tiers,)),
        ],
        compiler_params=pltpu.CompilerParams(
            collective_id=0, has_side_effects=True, vmem_limit_bytes=34 * 2**20
        ),
        name="electrothermal",
    )(
        *[pltpu.with_memory_space_constraint(x, pltpu.HBM) for x in (
            tap_index.reshape(tiers, 2, taps), tap_current.reshape(tiers, 2, taps), density, pad_cond, row_cond,
            col_cond, material, leak_rates, theta, kappa, invc,
        )],
    )


def solution(mesh):
    sizes = tuple(mesh.shape[name] for name in ("gx", "gy", "gz"))
    mesh_field = P("gz", "gx", "gy")
    tap = P("gz", "gx", "gy", None)
    block = P(None, "gx", ("gy", "gz"))
    return jax.shard_map(
        functools.partial(shards, sizes),
        mesh=mesh,
        in_specs=(mesh_field, tap, tap, mesh_field, mesh_field, mesh_field, mesh_field, P(), block, block, block),
        out_specs=(mesh_field, block),
        check_vma=False,
    )
```
